32 devices in a mesh: dp: 8 (over z, y), tensor: 4 (over x, core).
Axes of the slice: x: 2, y: 2, z: 4, core: 2. Of those that a mesh axis runs over, the one named last changes fastest.
Arguments:
- queries: bfloat16 [3072, 1536], P('dp', 'tensor'), may hold values from -6 to 6
- key_rows: bfloat16 [3072, 1536], P('dp', 'tensor'), may hold values from -6 to 6
- value_rows: bfloat16 [3072, 1536], P('dp', 'tensor'), may hold values from -6 to 6
- out_weight: bfloat16 [1536, 6144], P('tensor'), may hold values from -0.15625 to 0.15625
- segment_ids: int32 [8, 384], P('dp'), may hold values from 0 to 5, as said below
- move_flags: int32 [8, 384], P('dp'), may hold values from 0 to 1, as said below
- out_cotangent: bfloat16 [3584, 6144], P('dp', 'tensor'), may hold values from -6 to 6
Outputs:
- projected: bfloat16 [3584, 6144], P('dp', 'tensor')
- grad_queries: bfloat16 [3072, 1536], P('dp', 'tensor')
- grad_keys: bfloat16 [3072, 1536], P('dp', 'tensor')
- grad_values: bfloat16 [3072, 1536], P('dp', 'tensor')
The draws below stay inside these ranges and needn't reach their ends.
Inputs may be any that keep to these rules, and one draw needn't show every extreme that they name: `segment_ids`: in each data group the image numbers start at 0 and rise by 0 or 1 from row to row; a new image can begin only at a row that is a multiple of 64, and one always begins at row 320; in every draw some group reaches the largest number. `move_flags`: the images that one data group hands on hold at most 64 rows together; in every draw some group hands on exactly 64 rows and the group after it keeps all of its images.
All inputs are finite; a program needn't handle non-finite values.
Results may differ from the reference program's by a relative error of at most 0.015.
Values may be sent and summed in bfloat16 or wider, within the bound.
No kernel may reach another device: no remote copies, remote signals or barrier semaphores. Data moves between devices by JAX's collectives and lax.ppermute only.
A program may use at most 64 MiB of HBM per device.

```python
import jax
import jax.numpy as jnp
from jax import lax

D = 6144
HEAD = 128
HEADS = 12
HOME = 384
CAP = 64
DEST = 448
N_DP = 8
N_TENSOR = 4


def image_numbers(key):
    blocks = HOME // CAP
    starts_raw = jax.random.randint(jax.random.fold_in(key, 11), (N_DP, blocks), 0, 2)
    finest = jax.random.randint(jax.random.fold_in(key, 12), (), 0, N_DP)
    column = jnp.arange(HOME)[None, :]
    block_of = jnp.arange(HOME) // CAP
    group = jnp.arange(N_DP)[:, None]
    raw_rows = jnp.take(starts_raw, block_of, axis=1)
    on_grid = column % CAP == 0
    starts = on_grid & ((raw_rows == 0) | (column == 0) | (column == HOME - CAP) | (group == finest))
    return (jnp.cumsum(starts.astype(jnp.int32), axis=1) - 1).astype(jnp.int32)


def draw_segment_ids(key, part):
    numbers = image_numbers(key)
    return numbers


def draw_move_flags(key, part):
    numbers = image_numbers(key)
    key = jax.random.fold_in(key, 2)
    raw = jax.random.randint(key, (N_DP, HOME), 0, 2).astype(jnp.int32)
    row_flag = jnp.take_along_axis(raw, numbers, axis=1)
    running = jnp.cumsum(row_flag, axis=1)
    ends = jax.vmap(lambda c, s: jax.ops.segment_max(c, s, num_segments=HOME))(running, numbers)
    flags = raw * (ends <= CAP).astype(jnp.int32)
    full = jax.random.randint(jax.random.fold_in(key, 3), (), 0, N_DP)
    group = jnp.arange(N_DP)[:, None]
    image = jnp.arange(HOME)[None, :]
    first = numbers[:, HOME - CAP][:, None]
    full_row = (image >= first).astype(jnp.int32)
    flags = jnp.where(group == full, full_row, flags)
    flags = jnp.where(group == (full + 1) % N_DP, 0, flags)
    return flags.astype(jnp.int32)


def draw_queries(key, part):
    key = jax.random.fold_in(key, 5)
    rows = N_DP * HOME
    width = HEADS * HEAD
    base = jax.random.normal(key, (rows, width))
    return jnp.clip(base, -6.0, 6.0).astype(jnp.bfloat16)


def draw_key_rows(key, part):
    key = jax.random.fold_in(key, 6)
    rows = N_DP * HOME
    width = HEADS * HEAD
    base = jax.random.normal(key, (rows, width))
    return jnp.clip(base, -6.0, 6.0).astype(jnp.bfloat16)


def block_scale(own_key, extent, pieces, least, largest):
    level, own = 1.0, jax.random.fold_in(own_key, 6)
    for position, blocks in pieces:
        steps = jnp.exp(jax.random.uniform(jax.random.fold_in(own, position), (blocks,), jnp.float32, least / len(pieces), largest / len(pieces)))
        level = level * jnp.repeat(steps, extent[position] // blocks).reshape([-1 if axis == position else 1 for axis in range(len(extent))])
    return level


def normal_values(own_key, shape, deviation, limit, pieces=(), held_as=jnp.bfloat16):
    drawn = jax.random.normal(own_key, shape, jnp.float32) * deviation
    if len(pieces) > 0:
        drawn = block_scale(own_key, shape, pieces, -0.22, 0.18) * drawn
    return jnp.clip(drawn, min=-limit, max=limit).astype(held_as)


def setup_inputs(seed: int = 0) -> dict:
    splits = jax.random.split(jax.random.key(seed), 8)
    queries = draw_queries(jax.random.fold_in(splits[7], 71), 0)
    key_rows = draw_key_rows(jax.random.fold_in(splits[7], 71), 0)
    value_rows = normal_values(splits[2], (N_DP * HOME, HEADS * HEAD), 1.0, 6.0, ((0, 8), (1, 4)))
    out_weight = normal_values(splits[3], (HEADS * HEAD, D), (HEADS * HEAD) ** -0.5, 0.15625, ((0, 4),))
    segment_ids = draw_segment_ids(jax.random.fold_in(splits[7], 71), 0)
    move_flags = draw_move_flags(jax.random.fold_in(splits[7], 71), 0)
    out_cotangent = normal_values(splits[6], (N_DP * DEST, D), 1.0, 6.0, ((0, 8), (1, 4)))
    return dict(queries=queries, key_rows=key_rows, value_rows=value_rows, out_weight=out_weight, segment_ids=segment_ids, move_flags=move_flags, out_cotangent=out_cotangent)


def attend(query_wide, key_wide, value_wide, image_of):
    rows = query_wide.shape[0]
    heads = query_wide.shape[1] // HEAD
    qh = query_wide.reshape(rows, heads, HEAD)
    kh = key_wide.reshape(rows, heads, HEAD)
    vh = value_wide.reshape(rows, heads, HEAD)
    scores = jnp.einsum('qhd,khd->hqk', qh, kh) * HEAD ** (-0.5)
    same = image_of[:, None] == image_of[None, :]
    scores = jnp.where(same[None, :, :], scores, -1e+30)
    peak = lax.optimization_barrier(jnp.max(scores, axis=2, keepdims=True))
    weights = jnp.exp(scores - peak)
    weights = weights / lax.optimization_barrier(jnp.sum(weights, axis=2, keepdims=True))
    return jnp.einsum('hqk,khd->qhd', weights, vh).reshape(rows, heads * HEAD)

def reference(queries, key_rows, value_rows, out_weight, segment_ids, move_flags, out_cotangent):
    groups = N_DP
    width = HEADS * HEAD
    query_g = queries.reshape(groups, HOME, width)
    key_g = key_rows.reshape(groups, HOME, width)
    value_g = value_rows.reshape(groups, HOME, width)
    cot_g = out_cotangent.reshape(groups, DEST, D)
    row_move = jnp.take_along_axis(move_flags, segment_ids, axis=1).astype(jnp.int32)
    kept = (1 - row_move).astype(jnp.int32)
    kept_slot = (jnp.cumsum(kept, axis=1) - 1).astype(jnp.int32)
    move_slot = (jnp.cumsum(row_move, axis=1) - 1).astype(jnp.int32)
    kept_count = lax.optimization_barrier(jnp.sum(kept, axis=1)).astype(jnp.int32)
    weight_groups = out_weight.astype(jnp.float32).reshape(N_TENSOR, width // N_TENSOR, D)

    def forward_group(items):
        qg, kg, vg, sg = items
        attended = attend(qg.astype(jnp.float32), kg.astype(jnp.float32), vg.astype(jnp.float32), sg).astype(jnp.bfloat16)
        split = attended.astype(jnp.float32).reshape(HOME, N_TENSOR, width // N_TENSOR)
        partials = jnp.einsum('rtk,tkd->trd', split, weight_groups).astype(jnp.bfloat16)
        partials = lax.optimization_barrier(partials)
        return lax.optimization_barrier(jnp.sum(partials.astype(jnp.float32), axis=0)).astype(jnp.bfloat16)
    home_out = lax.map(forward_group, (query_g, key_g, value_g, segment_ids))
    kept_index = jnp.where(kept == 1, kept_slot, DEST).astype(jnp.int32)
    prev_out = jnp.roll(home_out, 1, axis=0)
    prev_move = jnp.roll(row_move, 1, axis=0)
    prev_slot = jnp.roll(move_slot, 1, axis=0)
    recv_index = jnp.where(prev_move == 1, kept_count[:, None] + prev_slot, DEST).astype(jnp.int32)

    def place(kept_rows, k_index, recv_rows, r_index):
        empty = jnp.zeros((DEST, kept_rows.shape[1]), jnp.bfloat16)
        empty = empty.at[k_index].set(kept_rows, mode='drop')
        return empty.at[r_index].set(recv_rows, mode='drop')
    projected = jax.vmap(place)(home_out, kept_index, prev_out, recv_index)
    next_cot = jnp.roll(cot_g, -1, axis=0)
    next_count = jnp.roll(kept_count, -1, axis=0)

    def pick(own_cot, far_cot, k_slot, m_slot, far_count, keep_row):
        from_own = jnp.take(own_cot, jnp.clip(k_slot, 0, DEST - 1), axis=0)
        from_far = jnp.take(far_cot, jnp.clip(far_count + m_slot, 0, DEST - 1), axis=0)
        return jnp.where(keep_row[:, None] == 1, from_own, from_far)
    home_cot = jax.vmap(pick)(cot_g, next_cot, kept_slot, move_slot, next_count, kept)

    def backward_group(items):
        qg, kg, vg, sg, cg = items
        attended_cot = jnp.dot(cg, out_weight.T, preferred_element_type=jnp.float32).astype(jnp.bfloat16)
        _, pull = jax.vjp(lambda a, b, c: attend(a, b, c, sg), qg.astype(jnp.float32), kg.astype(jnp.float32), vg.astype(jnp.float32))
        gq, gk, gv = pull(attended_cot.astype(jnp.float32))
        return (gq.astype(jnp.bfloat16), gk.astype(jnp.bfloat16), gv.astype(jnp.bfloat16))
    grad_q, grad_k, grad_v = lax.map(backward_group, (query_g, key_g, value_g, segment_ids, home_cot))
    return (projected.reshape(groups * DEST, D), grad_q.reshape(groups * HOME, width), grad_k.reshape(groups * HOME, width), grad_v.reshape(groups * HOME, width))
```

```python
import functools

import jax
import jax.numpy as jnp
from jax import lax
from jax.experimental import pallas as pl
from jax.experimental.pallas import tpu as pltpu
from jax.sharding import PartitionSpec as P

HEAD = 128
BF16 = jnp.bfloat16
F32 = jnp.float32
VMEM = pl.BlockSpec(memory_space=pltpu.VMEM)
SMEM = pl.BlockSpec(memory_space=pltpu.SMEM)
ANY = pl.BlockSpec(memory_space=pl.ANY)
LIMIT = 48 * 1024 * 1024


def nt(a, b):
    return lax.dot_general(a, b, (((1,), (1,)), ((), ())), preferred_element_type=F32)


def nn(a, b):
    return lax.dot_general(a, b, (((1,), (0,)), ((), ())), preferred_element_type=F32)


def tn(a, b):
    return lax.dot_general(a, b, (((0,), (0,)), ((), ())), preferred_element_type=F32)


def call(kernel, outs, ins, scratch=(), flops=0, moved=0, exps=0):
    return pl.pallas_call(
        kernel,
        out_shape=tuple(jax.ShapeDtypeStruct(s, t) for s, t in outs),
        in_specs=list(ins),
        out_specs=tuple(VMEM for _ in outs),
        scratch_shapes=list(scratch),
        compiler_params=pltpu.CompilerParams(vmem_limit_bytes=LIMIT),
        cost_estimate=pl.CostEstimate(flops=flops, bytes_accessed=moved, transcendentals=exps),
    )


def moved_block(seg, flags, blocks, cap):
    out = jnp.int32(blocks)
    for b in range(blocks):
        out = jnp.where(flags[0, seg[0, b * cap]] == 1, jnp.int32(b), out)
    return out


def forward_kernel(cap, seg, flags, q, k, v, att, sent, pt, rows_buf):
    rows, width = q.shape
    blocks = rows // cap
    gone = moved_block(seg, flags, blocks, cap)
    col_block = lax.broadcasted_iota(jnp.int32, (rows, 1), 0) // cap
    row_block = lax.broadcasted_iota(jnp.int32, (1, rows), 1) // cap
    key_id = jnp.zeros((rows, 1), jnp.int32)
    query_id = jnp.zeros((1, rows), jnp.int32)
    for b in range(blocks):
        image = seg[0, b * cap]
        key_id = jnp.where(col_block == b, image, key_id)
        query_id = jnp.where(row_block == b, image, query_id)
    same = key_id == query_id
    for h in range(width // HEAD):
        cols = slice(h * HEAD, (h + 1) * HEAD)
        scores = nt(k[:, cols], q[:, cols]) * HEAD ** (-0.5)
        scores = jnp.where(same, scores, -1e30)
        weights = jnp.exp(scores - jnp.max(scores, axis=0, keepdims=True))
        weights = weights * (1.0 / jnp.sum(weights, axis=0, keepdims=True))
        weights = weights.astype(BF16)
        pt[h] = weights
        out = tn(weights, v[:, cols]).astype(BF16)
        for b in range(blocks):
            slot = jnp.where(b < gone, b, jnp.where(b == gone, blocks, b - 1))
            rows_buf[slot, :, cols] = out[b * cap : (b + 1) * cap]
    empty = jnp.where(gone == blocks, blocks, blocks - 1)
    rows_buf[empty] = jnp.zeros((cap, width), BF16)
    for b in range(blocks):
        att[b * cap : (b + 1) * cap] = rows_buf[b]
    att[rows:] = jnp.zeros((cap, width), BF16)
    sent[...] = rows_buf[blocks]


def pick_kernel(cap, blocks, seg, flags, cot, out, sem):
    gone = moved_block(seg, flags, blocks, cap)
    start = pl.multiple_of(jnp.where(gone == blocks, blocks, blocks - 1) * cap, cap)
    copy = pltpu.make_async_copy(cot.at[pl.ds(start, cap), :], out, sem)
    copy.start()
    copy.wait()


def home_kernel(cap, blocks, seg, flags, cot, back, out, sems):
    gone = moved_block(seg, flags, blocks, cap)
    copies = []
    for b in range(blocks):
        start = pl.multiple_of((b - (b > gone).astype(jnp.int32)) * cap, cap)
        copies.append(
            pltpu.make_async_copy(
                cot.at[pl.ds(start, cap), :], out.at[pl.ds(b * cap, cap), :], sems.at[b]
            )
        )
    for c in copies:
        c.start()
    for c in copies:
        c.wait()

    @pl.when(gone < blocks)
    def _():
        start = pl.multiple_of(gone * cap, cap)
        copy = pltpu.make_async_copy(back, out.at[pl.ds(start, cap), :], sems.at[0])
        copy.start()
        copy.wait()


def own_kernel(ids, cot_own, cot_sib, weight, out, wbuf, sems):
    part = cot_own.shape[1]
    t = ids[0]
    copies = []
    for i in range(2):
        start = pl.multiple_of((t if i == 0 else t ^ 1) * part, part)
        copies.append(
            pltpu.make_async_copy(weight.at[:, pl.ds(start, part)], wbuf.at[i], sems.at[i])
        )
    for c in copies:
        c.start()
    copies[0].wait()
    out[...] = nt(cot_own[...], wbuf[0])
    copies[1].wait()
    out[...] += nt(cot_sib[...], wbuf[1])


def far_copies(ids, first, by_y, by_z, diag_a, diag_b, direct, wbuf, sems):
    place = ids[1]
    size, cols = first.shape
    half = size // 2
    top, low, whole = pl.ds(0, half), pl.ds(half, half), pl.ds(0, size)
    n = 0
    groups = []
    for share, pieces in (
        (place, ((first, whole),)),
        (place ^ 1, ((by_y, whole),)),
        (place ^ 2, ((by_z, whole),)),
        (place ^ 3, ((diag_a, top), (diag_b, low))),
    ):
        copies = []
        for src, where in pieces:
            copies.append(
                pltpu.make_async_copy(src, wbuf.at[share, where, :], sems.at[n])
            )
            n += 1
        start = pl.multiple_of(share * cols, cols)
        copies.append(
            pltpu.make_async_copy(
                direct.at[:, pl.ds(start, cols)],
                wbuf.at[share, pl.ds(size, direct.shape[0]), :],
                sems.at[n],
            )
        )
        n += 1
        groups.append((share, copies))
    return groups


def far_kernel(
    ids, cot_own, cot_sib, first, by_y, by_z, diag_a, diag_b, direct, out, wbuf, cbuf, sems, csems
):
    core = ids[0] & 1
    cols = wbuf.shape[2]
    loads = []
    for i, src in enumerate((cot_own, cot_sib)):
        for j in range(2):
            share = 2 * (core if i == 0 else 1 - core) + j
            loads.append(
                pltpu.make_async_copy(
                    src.at[:, pl.ds(j * cols, cols)], cbuf.at[share], csems.at[2 * i + j]
                )
            )
    groups = far_copies(ids, first, by_y, by_z, diag_a, diag_b, direct, wbuf, sems)
    for c in loads:
        c.start()
    for _, copies in groups:
        for c in copies:
            c.start()
    for c in loads:
        c.wait()
    total = None
    for share, copies in groups:
        for c in copies:
            c.wait()
        term = nt(cbuf[share], wbuf[share])
        total = term if total is None else total + term
    out[...] = total.astype(BF16)


def project_kernel(
    cap, seg, flags, ids, att, far_att, weight, first, by_y, by_z, diag_a, diag_b, direct,
    sib_out, own_out, left, wbuf, vbuf, sems, vsems,
):
    rows, width = att.shape
    blocks = rows // cap - 1
    t = ids[0]
    core = t & 1
    cols = wbuf.shape[2]
    groups = far_copies(ids, first, by_y, by_z, diag_a, diag_b, direct, wbuf, sems)
    loads = []
    for j in range(4):
        start = pl.multiple_of(((t >> 1) * 4 + j) * cols, cols)
        loads.append(
            pltpu.make_async_copy(weight.at[:, pl.ds(start, cols)], vbuf.at[j], vsems.at[j])
        )
    for c in loads:
        c.start()
    for _, copies in groups:
        for c in copies:
            c.start()
    gone = moved_block(seg, flags, blocks, cap)
    swap = gone < blocks
    last = (blocks - 1) * cap
    for i, src in enumerate((att, far_att)):
        where = slice(i * width, (i + 1) * width)
        left[:last, where] = src[:last]
        home, came = src[last:rows - cap], src[rows - cap :]
        left[last : rows - cap, where] = jnp.where(swap, came, home)
        left[rows - cap :, where] = jnp.where(swap, home, came)
    for c in loads:
        c.wait()
    for _, copies in groups:
        for c in copies:
            c.wait()
    for out, side in ((sib_out, 1 - core), (own_out, core)):
        for j in range(2):
            share = 2 * side + j
            term = nn(left[:, :width], vbuf[share]) + nn(left[:, width:], wbuf[share])
            out[:, j * cols : (j + 1) * cols] = term.astype(BF16)


def backward_kernel(q, k, v, pt, near, far, gq, gk, gv):
    for h in range(q.shape[1] // HEAD):
        cols = slice(h * HEAD, (h + 1) * HEAD)
        cot = (near[:, cols] + far[:, cols].astype(F32)).astype(BF16)
        weights = pt[h]
        gv[:, cols] = nn(weights, cot).astype(BF16)
        rise = nt(v[:, cols], cot)
        wide = weights.astype(F32)
        mean = jnp.sum(wide * rise, axis=0, keepdims=True)
        slope = (wide * (rise - mean) * HEAD ** (-0.5)).astype(BF16)
        gk[:, cols] = nn(slope, q[:, cols]).astype(BF16)
        gq[:, cols] = tn(slope, k[:, cols]).astype(BF16)


def flip(values, axis, by):
    size = lax.axis_size(axis)
    return lax.ppermute(values, axis, [(i, i ^ by) for i in range(size)])


def shifted(values, axis, by):
    size = lax.axis_size(axis)
    return lax.ppermute(values, axis, [(i, (i + by) % size) for i in range(size)])


def shards(queries, key_rows, value_rows, out_weight, segment_ids, move_flags, out_cotangent):
    home, width = queries.shape
    dest, part = out_cotangent.shape
    depth = out_weight.shape[1]
    cap = dest - home
    blocks = home // cap
    heads = width // HEAD
    t = lax.axis_index("tensor")
    place = lax.axis_index("dp") % 4
    ids = jnp.stack([t, place]).astype(jnp.int32)

    side_cols = depth // 2
    cols = side_cols // 4
    shared = (width * 3 // 4) // 32 * 32
    rest = width - shared
    far_side = (1 - t // 2) * side_cols
    share = lax.dynamic_slice(out_weight, (0, far_side + place * cols), (shared, cols))
    first = flip(share, "tensor", 2)

    scope = functools.partial(call)
    picked = scope(
        functools.partial(pick_kernel, cap, blocks),
        [((cap, part), BF16)],
        [SMEM, SMEM, ANY],
        [pltpu.SemaphoreType.DMA(())],
        moved=cap * part * 4,
    )(segment_ids, move_flags, out_cotangent)[0]
    back = shifted(picked, "dp", -1)

    att, sent, pt = scope(
        functools.partial(forward_kernel, cap),
        [((dest, width), BF16), ((cap, width), BF16), ((heads, home, home), BF16)],
        [SMEM, SMEM, VMEM, VMEM, VMEM],
        [pltpu.VMEM((blocks + 1, cap, width), BF16)],
        flops=4 * home * home * width,
        moved=5 * home * width * 2,
        exps=heads * home * home,
    )(segment_ids, move_flags, queries, key_rows, value_rows)
    came = shifted(sent, "dp", 1)

    by_y = flip(first, "dp", 1)
    by_z = flip(first, "dp", 2)
    direct = flip(
        lax.dynamic_slice(out_weight, (shared, far_side), (rest, side_cols)), "tensor", 2
    )

    cot_own = scope(
        functools.partial(home_kernel, cap, blocks),
        [((home, part), BF16)],
        [SMEM, SMEM, ANY, ANY],
        [pltpu.SemaphoreType.DMA((blocks,))],
        moved=home * part * 4,
    )(segment_ids, move_flags, out_cotangent, back)[0]
    cot_sib = flip(cot_own, "tensor", 1)

    half = shared // 2
    diag_a = flip(by_y[:half], "dp", 2)
    diag_b = flip(by_z[half:], "dp", 1)

    att = lax.dynamic_update_slice(att, came, (home, 0))
    far_att = flip(att, "tensor", 2)

    near = scope(
        own_kernel,
        [((home, width), F32)],
        [SMEM, VMEM, VMEM, ANY],
        [pltpu.VMEM((2, width, part), BF16), pltpu.SemaphoreType.DMA((2,))],
        flops=2 * home * width * side_cols,
        moved=(home + width) * side_cols * 2,
    )(ids, cot_own, cot_sib, out_weight)[0]

    pieces = (first, by_y, by_z, diag_a, diag_b, direct)
    send = scope(
        far_kernel,
        [((home, width), BF16)],
        [SMEM] + [ANY] * 8,
        [
            pltpu.VMEM((4, width, cols), BF16),
            pltpu.VMEM((4, home, cols), BF16),
            pltpu.SemaphoreType.DMA((9,)),
            pltpu.SemaphoreType.DMA((4,)),
        ],
        flops=2 * home * width * side_cols,
        moved=(home + width) * side_cols * 2,
    )(ids, cot_own, cot_sib, *pieces)[0]
    far = flip(send, "tensor", 2)

    sib_part, own_part = scope(
        functools.partial(project_kernel, cap),
        [((dest, part), BF16), ((dest, part), BF16)],
        [SMEM, SMEM, SMEM, VMEM, VMEM] + [ANY] * 7,
        [
            pltpu.VMEM((dest, 2 * width), BF16),
            pltpu.VMEM((4, width, cols), BF16),
            pltpu.VMEM((4, width, cols), BF16),
            pltpu.SemaphoreType.DMA((9,)),
            pltpu.SemaphoreType.DMA((4,)),
        ],
        flops=4 * dest * width * side_cols,
        moved=2 * width * side_cols * 2 + dest * side_cols * 2,
    )(segment_ids, move_flags, ids, att, far_att, out_weight, *pieces)
    other = flip(sib_part, "tensor", 1)
    projected = (own_part.astype(F32) + other.astype(F32)).astype(BF16)

    grad_q, grad_k, grad_v = scope(
        backward_kernel,
        [((home, width), BF16)] * 3,
        [VMEM] * 6,
        flops=8 * home * home * width,
        moved=9 * home * width * 2,
    )(queries, key_rows, value_rows, pt, near, far)
    return (projected, grad_q, grad_k, grad_v)


def wide_shards(queries, key_rows, value_rows, out_weight, segment_ids, move_flags, out_cotangent):
    home, width = queries.shape
    dest, part = out_cotangent.shape
    cap = dest - home
    blocks = home // cap
    heads = width // HEAD
    att, sent, pt = call(
        functools.partial(forward_kernel, cap),
        [((dest, width), BF16), ((cap, width), BF16), ((heads, home, home), BF16)],
        [SMEM, SMEM, VMEM, VMEM, VMEM],
        [pltpu.VMEM((blocks + 1, cap, width), BF16)],
    )(segment_ids, move_flags, queries, key_rows, value_rows)
    came = shifted(sent, "dp", 1)
    image_of = segment_ids[0, ::cap]
    gone = jnp.sum(jnp.take(move_flags[0], image_of))
    kept = home - gone * cap
    att = lax.dynamic_update_slice(att, came, (kept, 0))
    term = jnp.dot(att, out_weight, preferred_element_type=F32).astype(BF16)
    projected = lax.psum_scatter(term, "tensor", scatter_dimension=1, tiled=True)
    picked = lax.dynamic_slice(out_cotangent, (kept, 0), (cap, part))
    back = shifted(picked, "dp", -1)
    cot = call(
        functools.partial(home_kernel, cap, blocks),
        [((home, part), BF16)],
        [SMEM, SMEM, ANY, ANY],
        [pltpu.SemaphoreType.DMA((blocks,))],
    )(segment_ids, move_flags, out_cotangent, back)[0]
    whole = lax.all_gather(cot, "tensor", axis=1, tiled=True)
    near = nt(whole, out_weight)
    grad_q, grad_k, grad_v = call(
        backward_kernel, [((home, width), BF16)] * 3, [VMEM] * 6
    )(queries, key_rows, value_rows, pt, near, jnp.zeros((home, width), BF16))
    return (projected, grad_q, grad_k, grad_v)


def solution(mesh):
    square = mesh.shape["tensor"] == 4 and mesh.shape["dp"] % 4 == 0
    in_specs = (
        P("dp", "tensor"),
        P("dp", "tensor"),
        P("dp", "tensor"),
        P("tensor", None),
        P("dp", None),
        P("dp", None),
        P("dp", "tensor"),
    )
    out_specs = (P("dp", "tensor"), P("dp", "tensor"), P("dp", "tensor"), P("dp", "tensor"))
    return jax.shard_map(
        shards if square else wide_shards,
        mesh=mesh,
        in_specs=in_specs,
        out_specs=out_specs,
        check_vma=False,
    )
```

```python
import functools

import jax
import jax.numpy as jnp
from jax import lax
from jax.experimental import pallas as pl
from jax.experimental.pallas import tpu as pltpu
from jax.sharding import PartitionSpec as P

HEAD = 128
BF16 = jnp.bfloat16
F32 = jnp.float32
VMEM = pl.BlockSpec(memory_space=pltpu.VMEM)
SMEM = pl.BlockSpec(memory_space=pltpu.SMEM)
ANY = pl.BlockSpec(memory_space=pl.ANY)
LIMIT = 16 * 1024 * 1024
OPEN_LIMIT = 60 * 1024 * 1024


def nt(a, b):
    return lax.dot_general(a, b, (((1,), (1,)), ((), ())), preferred_element_type=F32)


def nn(a, b):
    return lax.dot_general(a, b, (((1,), (0,)), ((), ())), preferred_element_type=F32)


def tn(a, b):
    return lax.dot_general(a, b, (((0,), (0,)), ((), ())), preferred_element_type=F32)


def call(kernel, outs, ins, scratch=(), flops=0, moved=0, exps=0, limit=LIMIT):
    return pl.pallas_call(
        kernel,
        out_shape=tuple(jax.ShapeDtypeStruct(s, t) for s, t in outs),
        in_specs=list(ins),
        out_specs=tuple(SMEM if t == jnp.int32 else VMEM for _, t in outs),
        scratch_shapes=list(scratch),
        compiler_params=pltpu.CompilerParams(vmem_limit_bytes=limit),
        cost_estimate=pl.CostEstimate(flops=flops, bytes_accessed=moved, transcendentals=exps),
    )


def moved_block(seg, flags, blocks, cap):
    out = jnp.int32(blocks)
    for b in range(blocks):
        out = jnp.where(flags[0, seg[0, b * cap]] == 1, jnp.int32(b), out)
    return out


def forward_kernel(cap, seg, gone_ref, q, k, v, att, sent, pt, rows_buf):
    rows, width = q.shape
    blocks = rows // cap
    gone = gone_ref[0]
    col_block = lax.broadcasted_iota(jnp.int32, (rows, 1), 0) // cap
    row_block = lax.broadcasted_iota(jnp.int32, (1, rows), 1) // cap
    key_id = jnp.zeros((rows, 1), jnp.int32)
    query_id = jnp.zeros((1, rows), jnp.int32)
    for b in range(blocks):
        image = seg[0, b * cap]
        key_id = jnp.where(col_block == b, image, key_id)
        query_id = jnp.where(row_block == b, image, query_id)
    same = key_id == query_id
    for h in range(width // HEAD):
        cols = slice(h * HEAD, (h + 1) * HEAD)
        scores = nt(k[:, cols], q[:, cols]) * HEAD ** (-0.5)
        scores = jnp.where(same, scores, -1e30)
        weights = jnp.exp(scores - jnp.max(scores, axis=0, keepdims=True))
        weights = weights * (1.0 / jnp.sum(weights, axis=0, keepdims=True))
        weights = weights.astype(BF16)
        pt[h] = weights
        out = tn(weights, v[:, cols]).astype(BF16)
        for b in range(blocks):
            slot = jnp.where(b < gone, b, jnp.where(b == gone, blocks, b - 1))
            rows_buf[slot, :, cols] = out[b * cap : (b + 1) * cap]
    empty = jnp.where(gone == blocks, blocks, blocks - 1)
    rows_buf[empty] = jnp.zeros((cap, width), BF16)
    for b in range(blocks):
        att[b * cap : (b + 1) * cap] = rows_buf[b]
    att[rows:] = jnp.zeros((cap, width), BF16)
    sent[...] = rows_buf[blocks]


def open_kernel(
    cap, blocks, seg, flags, t, place, weight, cot, gone_out, share_out, direct_out, picked_out, sems
):
    cols = share_out.shape[1]
    rest = direct_out.shape[1] // 2
    part = cot.shape[1]
    far = (1 - (t[0] >> 1)) * 2 * part
    start = pl.multiple_of(far + (place[0] >> 1) * part + (place[0] & 1) * cols, HEAD)
    copies = [pltpu.make_async_copy(weight.at[:, pl.ds(start, cols)], share_out, sems.at[0])]
    for k in range(2):
        start = pl.multiple_of(far + k * part + 2 * cols, HEAD)
        copies.append(
            pltpu.make_async_copy(
                weight.at[:, pl.ds(start, rest)],
                direct_out.at[:, pl.ds(k * rest, rest)],
                sems.at[1 + k],
            )
        )
    for c in copies:
        c.start()
    gone = moved_block(seg, flags, blocks, cap)
    gone_out[0] = gone
    row = pl.multiple_of(jnp.where(gone == blocks, blocks, blocks - 1) * cap, cap)
    copies.append(pltpu.make_async_copy(cot.at[pl.ds(row, cap), :], picked_out, sems.at[3]))
    copies[-1].start()
    for c in copies:
        c.wait()


def pick_kernel(cap, blocks, seg, flags, cot, gone_out, picked_out):
    gone = moved_block(seg, flags, blocks, cap)
    gone_out[0] = gone
    row = jnp.where(gone == blocks, blocks, blocks - 1)
    picked_out[...] = cot[pl.ds(pl.multiple_of(row * cap, cap), cap), :]


def home_kernel(cap, blocks, gone_ref, *refs):
    gone = gone_ref[0]
    n = len(refs) // 3
    cots, backs, outs = refs[:n], refs[n : 2 * n], refs[2 * n :]
    for cot, out in zip(cots, outs):
        for b in range(blocks):
            start = pl.multiple_of((b - (b > gone).astype(jnp.int32)) * cap, cap)
            out[b * cap : (b + 1) * cap] = cot[pl.ds(start, cap), :]

    @pl.when(gone < blocks)
    def _():
        for back, out in zip(backs, outs):
            out[pl.ds(pl.multiple_of(gone * cap, cap), cap), :] = back[...]


def own_kernel(t_ref, cot_own, cot_sib, weight, out):
    part = cot_own.shape[1]
    t = t_ref[0]
    total = None
    for cot, i in ((cot_own, t), (cot_sib, t ^ 1)):
        start = pl.multiple_of(i * part, part)
        term = nt(cot[...], weight[:, pl.ds(start, part)])
        total = term if total is None else total + term
    out[...] = total


def by_place(t, place, own, sib, run):
    same = (t & 1) == (place >> 1)
    pl.when(same)(lambda: run(own, sib))
    pl.when(jnp.logical_not(same))(lambda: run(sib, own))


def far_kernel(t, place, cot_own, cot_sib, first, by_y, by_z, out):
    cols = first.shape[1]
    y = place[0] & 1
    near_at = pl.ds(pl.multiple_of(y * cols, HEAD), cols)
    next_at = pl.ds(pl.multiple_of((1 - y) * cols, HEAD), cols)

    def run(a, b):
        out[...] = (
            nt(a[:, near_at], first[...])
            + nt(a[:, next_at], by_y[...])
            + nt(b[:, near_at], by_z[...])
        )

    by_place(t[0], place[0], cot_own, cot_sib, run)


def last_kernel(t, place, cot_own, cot_sib, part_sum, diag_a, diag_b, direct, out):
    wide_a, wide_b = diag_a.shape[1], diag_b.shape[1]
    cols = wide_a + wide_b
    rest = direct.shape[1] // 2
    y = place[0] & 1
    core = t[0] & 1
    a_at = pl.ds(pl.multiple_of((1 - y) * cols, HEAD), wide_a)
    b_at = pl.ds(pl.multiple_of((1 - y) * cols + wide_a, HEAD), wide_b)
    own_at = pl.ds(pl.multiple_of(core * rest, HEAD), rest)
    sib_at = pl.ds(pl.multiple_of((1 - core) * rest, HEAD), rest)

    def run(a, b):
        total = part_sum[...] + nt(b[:, a_at], diag_a[...]) + nt(b[:, b_at], diag_b[...])
        total += nt(cot_own[:, 2 * cols :], direct[:, own_at])
        total += nt(cot_sib[:, 2 * cols :], direct[:, sib_at])
        out[...] = total.astype(BF16)

    by_place(t[0], place[0], cot_own, cot_sib, run)


def project_kernel(
    cap, gone_ref, t_ref, place_ref, att, far_att, weight, first, by_y, by_z, diag_a, diag_b, direct,
    sib_out, own_out, left,
):
    rows, width = att.shape
    blocks = rows // cap - 1
    t, place = t_ref[0], place_ref[0]
    core = t & 1
    y = place & 1
    z = place >> 1
    part = own_out.shape[1]
    cols = first.shape[1]
    wide_a = diag_a.shape[1]
    rest = direct.shape[1] // 2
    swap = gone_ref[0] < blocks
    last = (blocks - 1) * cap
    for i, src in enumerate((att, far_att)):
        where = slice(i * width, (i + 1) * width)
        left[:last, where] = src[:last]
        home, came = src[last : rows - cap, :], src[rows - cap :, :]
        left[last : rows - cap, where] = jnp.where(swap, came, home)
        left[rows - cap :, where] = jnp.where(swap, home, came)

    def put(out, k, at, size, far_weight):
        start = pl.multiple_of((t >> 1) * 2 * part + k * part + at, HEAD)
        both = jnp.concatenate([weight[:, pl.ds(start, size)], far_weight], axis=0)
        term = nn(left[...], both)
        out[:, pl.ds(pl.multiple_of(at, HEAD), size)] = term.astype(BF16)

    def run(a, b):
        put(a, z, y * cols, cols, first[...])
        put(a, z, (1 - y) * cols, cols, by_y[...])
        put(b, 1 - z, y * cols, cols, by_z[...])
        put(b, 1 - z, (1 - y) * cols, wide_a, diag_a[...])
        put(b, 1 - z, (1 - y) * cols + wide_a, cols - wide_a, diag_b[...])

    by_place(t, place, own_out, sib_out, run)
    for out, k in ((sib_out, 1 - core), (own_out, core)):
        at = pl.ds(pl.multiple_of(k * rest, HEAD), rest)
        put(out, k, 2 * cols, rest, direct[:, at])


def backward_kernel(q, k, v, pt, near, far, gq, gk, gv):
    for h in range(q.shape[1] // HEAD):
        cols = slice(h * HEAD, (h + 1) * HEAD)
        cot = (near[:, cols] + far[:, cols].astype(F32)).astype(BF16)
        weights = pt[h]
        gv[:, cols] = nn(weights, cot).astype(BF16)
        rise = nt(v[:, cols], cot)
        wide = weights.astype(F32)
        mean = jnp.sum(wide * rise, axis=0, keepdims=True)
        slope = (wide * (rise - mean) * HEAD ** (-0.5)).astype(BF16)
        gk[:, cols] = nn(slope, q[:, cols]).astype(BF16)
        gq[:, cols] = tn(slope, k[:, cols]).astype(BF16)


def flip(values, axis, by):
    size = lax.axis_size(axis)
    return lax.ppermute(values, axis, [(i, i ^ by) for i in range(size)])


def shifted(values, axis, by):
    size = lax.axis_size(axis)
    return lax.ppermute(values, axis, [(i, (i + by) % size) for i in range(size)])


def tie(value, *others):
    return lax.optimization_barrier((value, *others))[0]


def shards(queries, key_rows, value_rows, out_weight, segment_ids, move_flags, out_cotangent):
    home, width = queries.shape
    dest, part = out_cotangent.shape
    cap = dest - home
    blocks = home // cap
    heads = width // HEAD
    cols = part * 5 // 12 // HEAD * HEAD
    rest = part - 2 * cols
    wide_a = (cols + HEAD) // 2 // HEAD * HEAD
    t = lax.axis_index("tensor").astype(jnp.int32).reshape(1)
    place = (lax.axis_index("dp").astype(jnp.int32) & 3).reshape(1)

    gone, share, direct, picked = call(
        functools.partial(open_kernel, cap, blocks),
        [
            ((1,), jnp.int32),
            ((width, cols), BF16),
            ((width, 2 * rest), BF16),
            ((cap, part), BF16),
        ],
        [SMEM, SMEM, SMEM, SMEM, ANY, ANY],
        [pltpu.SemaphoreType.DMA((4,))],
        limit=OPEN_LIMIT,
    )(segment_ids, move_flags, t, place, out_weight, out_cotangent)
    first = flip(share, "tensor", 2)
    cot_raw = flip(out_cotangent, "tensor", 1)
    back = shifted(picked, "dp", -1)

    att, sent, pt = call(
        functools.partial(forward_kernel, cap),
        [((dest, width), BF16), ((cap, width), BF16), ((heads, home, home), BF16)],
        [SMEM, SMEM, VMEM, VMEM, VMEM],
        [pltpu.VMEM((blocks + 1, cap, width), BF16)],
    )(segment_ids, gone, queries, key_rows, value_rows)
    came = shifted(sent, "dp", 1)
    back_sib = flip(tie(back, sent), "tensor", 1)

    first, back_sib, cot_raw, sent = lax.optimization_barrier((first, back_sib, cot_raw, sent))
    by_y = flip(first, "dp", 1)
    by_z = flip(first, "dp", 2)
    direct = flip(tie(direct, first), "tensor", 2)

    cot_own, cot_sib = call(
        functools.partial(home_kernel, cap, blocks),
        [((home, part), BF16)] * 2,
        [SMEM] + [VMEM] * 4,
    )(gone, out_cotangent, cot_raw, back, back_sib)

    near = call(
        own_kernel,
        [((home, width), F32)],
        [SMEM, VMEM, VMEM, VMEM],
        flops=4 * home * width * part,
        moved=(home + width) * part * 4,
    )(t, cot_own, cot_sib, out_weight)[0]

    by_y, by_z, near = lax.optimization_barrier((by_y, by_z, near))
    cut_a, cut_b = lax.optimization_barrier((by_y[:, :wide_a], by_z[:, wide_a:]))
    diag_a = flip(cut_a, "dp", 2)
    diag_b = flip(cut_b, "dp", 1)

    att = lax.dynamic_update_slice(att, came, (home, 0))
    far_att = flip(att, "tensor", 2)

    half = call(
        far_kernel,
        [((home, width), F32)],
        [SMEM, SMEM] + [VMEM] * 5,
        flops=6 * home * width * cols,
        moved=(home + width) * cols * 6,
    )(t, place, cot_own, cot_sib, first, by_y, by_z)[0]
    send = call(
        last_kernel,
        [((home, width), BF16)],
        [SMEM, SMEM] + [VMEM] * 6,
        flops=2 * home * width * (cols + 2 * rest),
        moved=(home + width) * (cols + 2 * rest) * 2,
    )(t, place, cot_own, cot_sib, half, diag_a, diag_b, direct)[0]
    far = flip(send, "tensor", 2)

    sib_part, own_part = call(
        functools.partial(project_kernel, cap),
        [((dest, part), BF16), ((dest, part), BF16)],
        [SMEM] * 3 + [VMEM] * 9,
        [pltpu.VMEM((dest, 2 * width), BF16)],
        flops=8 * dest * width * part,
        moved=8 * width * part + dest * part * 4,
    )(gone, t, tie(place, send), att, far_att, out_weight, first, by_y, by_z, diag_a, diag_b, direct)
    other = flip(sib_part, "tensor", 1)
    projected = (own_part.astype(F32) + other.astype(F32)).astype(BF16)

    grad_q, grad_k, grad_v = call(
        backward_kernel,
        [((home, width), BF16)] * 3,
        [VMEM] * 6,
        flops=3200 * home * home * width,
        moved=9 * home * width * 2,
    )(queries, key_rows, value_rows, pt, near, far)
    return (projected, grad_q, grad_k, grad_v)


def wide_shards(queries, key_rows, value_rows, out_weight, segment_ids, move_flags, out_cotangent):
    home, width = queries.shape
    dest, part = out_cotangent.shape
    cap = dest - home
    blocks = home // cap
    heads = width // HEAD
    gone, picked = call(
        functools.partial(pick_kernel, cap, blocks),
        [((1,), jnp.int32), ((cap, part), BF16)],
        [SMEM, SMEM, VMEM],
    )(segment_ids, move_flags, out_cotangent)
    att, sent, pt = call(
        functools.partial(forward_kernel, cap),
        [((dest, width), BF16), ((cap, width), BF16), ((heads, home, home), BF16)],
        [SMEM, SMEM, VMEM, VMEM, VMEM],
        [pltpu.VMEM((blocks + 1, cap, width), BF16)],
    )(segment_ids, gone, queries, key_rows, value_rows)
    came = shifted(sent, "dp", 1)
    kept = jnp.where(gone[0] < blocks, home - cap, home)
    att = lax.dynamic_update_slice(att, came, (kept, 0))
    term = jnp.dot(att, out_weight, preferred_element_type=F32).astype(BF16)
    projected = lax.psum_scatter(term, "tensor", scatter_dimension=1, tiled=True)
    back = shifted(picked, "dp", -1)
    cot = call(
        functools.partial(home_kernel, cap, blocks),
        [((home, part), BF16)],
        [SMEM, VMEM, VMEM],
    )(gone, out_cotangent, back)[0]
    whole = lax.all_gather(cot, "tensor", axis=1, tiled=True)
    near = nt(whole, out_weight)
    grad_q, grad_k, grad_v = call(
        backward_kernel, [((home, width), BF16)] * 3, [VMEM] * 6
    )(queries, key_rows, value_rows, pt, near, jnp.zeros((home, width), BF16))
    return (projected, grad_q, grad_k, grad_v)


def solution(mesh):
    square = mesh.shape["tensor"] == 4 and mesh.shape["dp"] % 4 == 0
    in_specs = (
        P("dp", "tensor"),
        P("dp", "tensor"),
        P("dp", "tensor"),
        P("tensor", None),
        P("dp", None),
        P("dp", None),
        P("dp", "tensor"),
    )
    out_specs = (P("dp", "tensor"), P("dp", "tensor"), P("dp", "tensor"), P("dp", "tensor"))
    return jax.shard_map(
        shards if square else wide_shards,
        mesh=mesh,
        in_specs=in_specs,
        out_specs=out_specs,
        check_vma=False,
    )
```

```python
import functools

import jax
import jax.numpy as jnp
from jax import lax
from jax.experimental import pallas as pl
from jax.experimental.pallas import tpu as pltpu
from jax.sharding import PartitionSpec as P

HEAD = 128
BF16 = jnp.bfloat16
F32 = jnp.float32
VMEM = pl.BlockSpec(memory_space=pltpu.VMEM)
SMEM = pl.BlockSpec(memory_space=pltpu.SMEM)
ANY = pl.BlockSpec(memory_space=pl.ANY)
LIMIT = 16 * 1024 * 1024
OPEN_LIMIT = 52 * 1024 * 1024


def nt(a, b):
    return lax.dot_general(a, b, (((1,), (1,)), ((), ())), preferred_element_type=F32)


def nn(a, b):
    return lax.dot_general(a, b, (((1,), (0,)), ((), ())), preferred_element_type=F32)


def tn(a, b):
    return lax.dot_general(a, b, (((0,), (0,)), ((), ())), preferred_element_type=F32)


def call(kernel, outs, ins, scratch=(), flops=0, moved=0, exps=0, limit=LIMIT):
    return pl.pallas_call(
        kernel,
        out_shape=tuple(jax.ShapeDtypeStruct(s, t) for s, t in outs),
        in_specs=list(ins),
        out_specs=tuple(SMEM if t == jnp.int32 else VMEM for _, t in outs),
        scratch_shapes=list(scratch),
        compiler_params=pltpu.CompilerParams(vmem_limit_bytes=limit),
        cost_estimate=pl.CostEstimate(flops=flops, bytes_accessed=moved, transcendentals=exps),
    )


def moved_block(seg, flags, blocks, cap):
    out = jnp.int32(blocks)
    for b in range(blocks):
        out = jnp.where(flags[0, seg[0, b * cap]] == 1, jnp.int32(b), out)
    return out


def attend(segment_ids, move_flags, queries, key_rows, value_rows, out_cotangent):
    home, width = queries.shape
    dest, part = out_cotangent.shape
    cap = dest - home
    return call(
        functools.partial(forward_kernel, cap),
        [
            ((1,), jnp.int32),
            ((cap, part), BF16),
            ((dest, width), BF16),
            ((cap, width), BF16),
            ((width // HEAD, home, home), BF16),
        ],
        [SMEM, SMEM] + [VMEM] * 4,
        [pltpu.VMEM((home // cap + 1, cap, width), BF16)],
    )(segment_ids, move_flags, queries, key_rows, value_rows, out_cotangent)


def forward_kernel(cap, seg, flags, q, k, v, cot, gone_out, picked, att, sent, pt, rows_buf):
    rows, width = q.shape
    blocks = rows // cap
    gone = moved_block(seg, flags, blocks, cap)
    gone_out[0] = gone
    row = jnp.where(gone == blocks, blocks, blocks - 1)
    picked[...] = cot[pl.ds(pl.multiple_of(row * cap, cap), cap), :]
    col_block = lax.broadcasted_iota(jnp.int32, (rows, 1), 0) // cap
    row_block = lax.broadcasted_iota(jnp.int32, (1, rows), 1) // cap
    key_id = jnp.zeros((rows, 1), jnp.int32)
    query_id = jnp.zeros((1, rows), jnp.int32)
    for b in range(blocks):
        image = seg[0, b * cap]
        key_id = jnp.where(col_block == b, image, key_id)
        query_id = jnp.where(row_block == b, image, query_id)
    same = key_id == query_id
    for h in range(width // HEAD):
        cols = slice(h * HEAD, (h + 1) * HEAD)
        scores = nt(k[:, cols], q[:, cols]) * HEAD ** (-0.5)
        scores = jnp.where(same, scores, -1e30)
        weights = jnp.exp(scores - jnp.max(scores, axis=0, keepdims=True))
        weights = weights * (1.0 / jnp.sum(weights, axis=0, keepdims=True))
        weights = weights.astype(BF16)
        pt[h] = weights
        out = tn(weights, v[:, cols]).astype(BF16)
        for b in range(blocks):
            slot = jnp.where(b < gone, b, jnp.where(b == gone, blocks, b - 1))
            rows_buf[slot, :, cols] = out[b * cap : (b + 1) * cap]
    empty = jnp.where(gone == blocks, blocks, blocks - 1)
    rows_buf[empty] = jnp.zeros((cap, width), BF16)
    for b in range(blocks):
        att[b * cap : (b + 1) * cap] = rows_buf[b]
    att[rows:] = jnp.zeros((cap, width), BF16)
    sent[...] = rows_buf[blocks]


def share_kernel(part, cols, t, place, weight, *refs):
    outs, direct, sems = refs[:-2], refs[-2], refs[-1]
    rest = direct.shape[1] // 2
    far = (1 - (t[0] >> 1)) * 2 * part
    at = far + (place[0] >> 1) * part + (place[0] & 1) * cols
    moves = []
    for out in outs:
        moves.append((at, out))
        at += out.shape[1]
    for k in range(2):
        moves.append((far + (k + 1) * part - rest, direct.at[:, pl.ds(k * rest, rest)]))
    copies = []
    for i, (start, out) in enumerate(moves):
        where = pl.ds(pl.multiple_of(start, HEAD), out.shape[1])
        copies.append(pltpu.make_async_copy(weight.at[:, where], out, sems.at[i]))
    for c in copies:
        c.start()
    for c in copies:
        c.wait()


def home_kernel(cap, blocks, gone_ref, *refs):
    gone = gone_ref[0]
    n = len(refs) // 3
    cots, backs, outs = refs[:n], refs[n : 2 * n], refs[2 * n :]
    for cot, out in zip(cots, outs):
        for b in range(blocks):
            start = pl.multiple_of((b - (b > gone).astype(jnp.int32)) * cap, cap)
            out[b * cap : (b + 1) * cap] = cot[pl.ds(start, cap), :]

    @pl.when(gone < blocks)
    def _():
        for back, out in zip(backs, outs):
            out[pl.ds(pl.multiple_of(gone * cap, cap), cap), :] = back[...]


def own_kernel(t_ref, cot_own, cot_sib, weight, out):
    part = cot_own.shape[1]
    t = t_ref[0]
    total = None
    for cot, i in ((cot_own, t), (cot_sib, t ^ 1)):
        start = pl.multiple_of(i * part, part)
        term = nt(cot[...], weight[:, pl.ds(start, part)])
        total = term if total is None else total + term
    out[...] = total


def by_place(t, place, own, sib, run):
    same = (t & 1) == (place >> 1)
    pl.when(same)(lambda: run(own, sib))
    pl.when(jnp.logical_not(same))(lambda: run(sib, own))


def far_kernel(t, place, cot_own, cot_sib, *refs):
    out, chunks = refs[-1], refs[:-1]
    chunks = [chunks[i : i + 3] for i in range(0, len(chunks), 3)]
    cols = sum(c[0].shape[1] for c in chunks)
    y = place[0] & 1

    def run(a, b):
        total = None
        at = 0
        for mine, by_y, by_z in chunks:
            size = mine.shape[1]
            near_at = pl.ds(pl.multiple_of(y * cols + at, HEAD), size)
            next_at = pl.ds(pl.multiple_of((1 - y) * cols + at, HEAD), size)
            term = nt(a[:, near_at], mine[...]) + nt(a[:, next_at], by_y[...])
            term += nt(b[:, near_at], by_z[...])
            total = term if total is None else total + term
            at += size
        out[...] = total

    by_place(t[0], place[0], cot_own, cot_sib, run)


def last_kernel(t, place, cot_own, cot_sib, part_sum, diag_a, diag_b, direct, out):
    wide_a, wide_b = diag_a.shape[1], diag_b.shape[1]
    cols = wide_a + wide_b
    rest = direct.shape[1] // 2
    y = place[0] & 1
    core = t[0] & 1
    a_at = pl.ds(pl.multiple_of((1 - y) * cols, HEAD), wide_a)
    b_at = pl.ds(pl.multiple_of((1 - y) * cols + wide_a, HEAD), wide_b)
    own_at = pl.ds(pl.multiple_of(core * rest, HEAD), rest)
    sib_at = pl.ds(pl.multiple_of((1 - core) * rest, HEAD), rest)

    def run(a, b):
        total = part_sum[...] + nt(b[:, a_at], diag_a[...]) + nt(b[:, b_at], diag_b[...])
        total += nt(cot_own[:, 2 * cols :], direct[:, own_at])
        total += nt(cot_sib[:, 2 * cols :], direct[:, sib_at])
        out[...] = total.astype(BF16)

    by_place(t[0], place[0], cot_own, cot_sib, run)


def fill_left(cap, gone, att, far_att, left):
    rows, width = att.shape
    last = rows - 2 * cap
    swap = gone * cap < rows - cap
    for i, src in enumerate((att, far_att)):
        where = slice(i * width, (i + 1) * width)
        left[:last, where] = src[:last]
        home, came = src[last : rows - cap, :], src[rows - cap :, :]
        left[last : rows - cap, where] = jnp.where(swap, came, home)
        left[rows - cap :, where] = jnp.where(swap, home, came)


def early_kernel(cap, part, gone, t_ref, place_ref, att, far_att, weight, *refs):
    own_out, sib_out, left = refs[-3:]
    chunks = [refs[i : i + 3] for i in range(0, len(refs) - 3, 3)]
    t, place = t_ref[0], place_ref[0]
    y, z = place & 1, place >> 1
    cols = own_out.shape[1] // 2
    fill_left(cap, gone[0], att, far_att, left)

    def run(a, b):
        at = 0
        for mine, by_y, by_z in chunks:
            size = mine.shape[1]
            for out, k, j, far_weight in (
                (a, z, y, mine),
                (a, z, 1 - y, by_y),
                (b, 1 - z, y, by_z),
            ):
                start = pl.multiple_of(((t >> 1) * 2 + k) * part + j * cols + at, HEAD)
                both = jnp.concatenate([weight[:, pl.ds(start, size)], far_weight[...]], axis=0)
                here = pl.ds(pl.multiple_of(j * cols + at, HEAD), size)
                out[:, here] = nn(left[...], both).astype(BF16)
            at += size

    by_place(t, place, own_out, sib_out, run)


def late_kernel(t_ref, place_ref, left, weight, diag_a, diag_b, direct, own_out, sib_out):
    t, place = t_ref[0], place_ref[0]
    core, y, z = t & 1, place & 1, place >> 1
    part = weight.shape[1] // 4
    cols = diag_a.shape[1] + diag_b.shape[1]
    rest = direct.shape[1] // 2

    def product(k, at, size, far_weight):
        start = pl.multiple_of(((t >> 1) * 2 + k) * part + at, HEAD)
        both = jnp.concatenate([weight[:, pl.ds(start, size)], far_weight], axis=0)
        return nn(left[...], both).astype(BF16)

    at = 0
    for piece in (diag_a, diag_b):
        size = piece.shape[1]
        value = product(1 - z, (1 - y) * cols + at, size, piece[...])
        own_out[:, at : at + size] = value
        sib_out[:, at : at + size] = value
        at += size
    for out, k in ((own_out, core), (sib_out, 1 - core)):
        where = pl.ds(pl.multiple_of(k * rest, HEAD), rest)
        out[:, cols:] = product(k, 2 * cols, rest, direct[:, where])


def join_kernel(t_ref, place_ref, own, other, own_late, other_late, out):
    t, place = t_ref[0], place_ref[0]
    y, z = place & 1, place >> 1
    cols = own.shape[1] // 2

    def add(a, b):
        return (a.astype(F32) + b.astype(F32)).astype(BF16)

    @pl.when((t & 1) == z)
    def _():
        out[:, : 2 * cols] = add(own[...], other[...])

    @pl.when((t & 1) != z)
    def _():
        here = pl.ds(pl.multiple_of(y * cols, HEAD), cols)
        out[:, here] = add(own[:, here], other[:, here])
        there = pl.ds(pl.multiple_of((1 - y) * cols, HEAD), cols)
        out[:, there] = add(own_late[:, :cols], other_late[:, :cols])

    out[:, 2 * cols :] = add(own_late[:, cols:], other_late[:, cols:])


def backward_kernel(q, k, v, pt, near, far, gq, gk, gv):
    for h in range(q.shape[1] // HEAD):
        cols = slice(h * HEAD, (h + 1) * HEAD)
        cot = (near[:, cols] + far[:, cols].astype(F32)).astype(BF16)
        weights = pt[h]
        gv[:, cols] = nn(weights, cot).astype(BF16)
        rise = nt(v[:, cols], cot)
        wide = weights.astype(F32)
        mean = jnp.sum(wide * rise, axis=0, keepdims=True)
        slope = (wide * (rise - mean) * HEAD ** (-0.5)).astype(BF16)
        gk[:, cols] = nn(slope, q[:, cols]).astype(BF16)
        gq[:, cols] = tn(slope, k[:, cols]).astype(BF16)


def flip(values, axis, by):
    size = lax.axis_size(axis)
    return lax.ppermute(values, axis, [(i, i ^ by) for i in range(size)])


def shifted(values, axis, by):
    size = lax.axis_size(axis)
    return lax.ppermute(values, axis, [(i, (i + by) % size) for i in range(size)])


def tie(value, *others):
    return lax.optimization_barrier((value, *others))[0]


def shards(queries, key_rows, value_rows, out_weight, segment_ids, move_flags, out_cotangent):
    home, width = queries.shape
    dest, part = out_cotangent.shape
    cap = dest - home
    blocks = home // cap
    heads = width // HEAD
    cols = part * 5 // 12 // HEAD * HEAD
    rest = part - 2 * cols
    wide_a = (cols + HEAD) // 2 // HEAD * HEAD
    t = lax.axis_index("tensor").astype(jnp.int32).reshape(1)
    place = (lax.axis_index("dp").astype(jnp.int32) & 3).reshape(1)

    share, direct = call(
        functools.partial(share_kernel, part, cols),
        [((width, cols), BF16), ((width, 2 * rest), BF16)],
        [SMEM, SMEM, ANY],
        [pltpu.SemaphoreType.DMA((3,))],
        limit=OPEN_LIMIT,
    )(t, place, out_weight)
    first = flip(share, "tensor", 2)
    cot_raw = flip(out_cotangent, "tensor", 1)

    gone, picked, att, sent, pt = attend(
        tie(segment_ids, share), move_flags, queries, key_rows, value_rows, out_cotangent
    )
    back = shifted(picked, "dp", -1)
    came = shifted(sent, "dp", 1)

    first, back, came = lax.optimization_barrier((first, back, came))
    by_y = flip(first, "dp", 1)
    by_z = flip(first, "dp", 2)
    att = lax.dynamic_update_slice(att, came, (home, 0))
    far_att = flip(att, "tensor", 2)
    direct = flip(tie(direct, att), "tensor", 2)
    back_sib = flip(back, "tensor", 1)

    cot_own, cot_sib = call(
        functools.partial(home_kernel, cap, blocks),
        [((home, part), BF16)] * 2,
        [SMEM] + [VMEM] * 4,
    )(gone, out_cotangent, cot_raw, back, back_sib)

    near = call(
        own_kernel,
        [((home, width), F32)],
        [SMEM, VMEM, VMEM, VMEM],
        flops=4 * home * width * part,
        moved=(home + width) * part * 4,
    )(t, cot_own, cot_sib, out_weight)[0]

    by_y, by_z, near, far_att = lax.optimization_barrier((by_y, by_z, near, far_att))
    diag_a = flip(by_y[:, :wide_a], "dp", 2)
    diag_b = flip(by_z[:, wide_a:], "dp", 1)

    early = (first, by_y, by_z)
    half = call(
        far_kernel,
        [((home, width), F32)],
        [SMEM, SMEM] + [VMEM] * 5,
        flops=6 * home * width * cols,
        moved=(home + width) * cols * 6,
    )(t, place, cot_own, cot_sib, *early)[0]
    own, sib, left = call(
        functools.partial(early_kernel, cap, part),
        [((dest, 2 * cols), BF16), ((dest, 2 * cols), BF16), ((dest, 2 * width), BF16)],
        [SMEM] * 3 + [VMEM] * 6,
        flops=12 * dest * width * cols,
        moved=12 * width * cols + dest * part * 4,
    )(gone, t, place, att, far_att, out_weight, *early)
    other = flip(sib, "tensor", 1)
    half, own, near = lax.optimization_barrier((half, own, near))
    send = call(
        last_kernel,
        [((home, width), BF16)],
        [SMEM, SMEM] + [VMEM] * 6,
        flops=2 * home * width * (cols + 2 * rest),
        moved=(home + width) * (cols + 2 * rest) * 2,
    )(t, place, cot_own, cot_sib, half, diag_a, diag_b, direct)[0]
    far = flip(send, "tensor", 2)
    own_late, sib_late = call(
        late_kernel,
        [((dest, cols + rest), BF16)] * 2,
        [SMEM] * 2 + [VMEM] * 5,
        flops=4 * dest * width * (cols + 2 * rest),
        moved=4 * width * (cols + 2 * rest) + dest * part * 2,
    )(t, tie(place, send), left, out_weight, diag_a, diag_b, direct)
    other_late = flip(sib_late, "tensor", 1)
    projected = call(
        join_kernel,
        [((dest, part), BF16)],
        [SMEM] * 2 + [VMEM] * 4,
        moved=dest * part * 6,
    )(t, place, own, other, own_late, other_late)[0]

    grad_q, grad_k, grad_v = call(
        backward_kernel,
        [((home, width), BF16)] * 3,
        [VMEM] * 6,
        flops=800 * home * home * width,
        moved=9 * home * width * 2,
    )(queries, key_rows, value_rows, pt, near, far)
    return (projected, grad_q, grad_k, grad_v)


def wide_shards(queries, key_rows, value_rows, out_weight, segment_ids, move_flags, out_cotangent):
    home, width = queries.shape
    dest, part = out_cotangent.shape
    cap = dest - home
    blocks = home // cap
    heads = width // HEAD
    gone, picked, att, sent, pt = attend(
        segment_ids, move_flags, queries, key_rows, value_rows, out_cotangent
    )
    came = shifted(sent, "dp", 1)
    kept = jnp.where(gone[0] < blocks, home - cap, home)
    att = lax.dynamic_update_slice(att, came, (kept, 0))
    term = jnp.dot(att, out_weight, preferred_element_type=F32).astype(BF16)
    projected = lax.psum_scatter(term, "tensor", scatter_dimension=1, tiled=True)
    back = shifted(picked, "dp", -1)
    cot = call(
        functools.partial(home_kernel, cap, blocks),
        [((home, part), BF16)],
        [SMEM, VMEM, VMEM],
    )(gone, out_cotangent, back)[0]
    whole = lax.all_gather(cot, "tensor", axis=1, tiled=True)
    near = nt(whole, out_weight)
    grad_q, grad_k, grad_v = call(
        backward_kernel, [((home, width), BF16)] * 3, [VMEM] * 6
    )(queries, key_rows, value_rows, pt, near, jnp.zeros((home, width), BF16))
    return (projected, grad_q, grad_k, grad_v)


def solution(mesh):
    square = mesh.shape["tensor"] == 4 and mesh.shape["dp"] % 4 == 0
    in_specs = (
        P("dp", "tensor"),
        P("dp", "tensor"),
        P("dp", "tensor"),
        P("tensor", None),
        P("dp", None),
        P("dp", None),
        P("dp", "tensor"),
    )
    out_specs = (P("dp", "tensor"), P("dp", "tensor"), P("dp", "tensor"), P("dp", "tensor"))
    return jax.shard_map(
        shards if square else wide_shards,
        mesh=mesh,
        in_specs=in_specs,
        out_specs=out_specs,
        check_vma=False,
    )
```

```python
import functools

import jax
import jax.numpy as jnp
from jax import lax
from jax.experimental import pallas as pl
from jax.experimental.pallas import tpu as pltpu
from jax.sharding import PartitionSpec as P

HEAD = 128
BF16 = jnp.bfloat16
F32 = jnp.float32
VMEM = pl.BlockSpec(memory_space=pltpu.VMEM)
SMEM = pl.BlockSpec(memory_space=pltpu.SMEM)
ANY = pl.BlockSpec(memory_space=pl.ANY)
LIMIT = 16 * 1024 * 1024
OPEN_LIMIT = 52 * 1024 * 1024


def nt(a, b):
    return lax.dot_general(a, b, (((1,), (1,)), ((), ())), preferred_element_type=F32)


def nn(a, b):
    return lax.dot_general(a, b, (((1,), (0,)), ((), ())), preferred_element_type=F32)


def tn(a, b):
    return lax.dot_general(a, b, (((0,), (0,)), ((), ())), preferred_element_type=F32)


def call(kernel, outs, ins, scratch=(), flops=0, moved=0, exps=0, limit=LIMIT, out=None):
    return pl.pallas_call(
        kernel,
        out_shape=tuple(jax.ShapeDtypeStruct(s, t) for s, t in outs),
        in_specs=list(ins),
        out_specs=tuple(out or (SMEM if t == jnp.int32 else VMEM) for _, t in outs),
        scratch_shapes=list(scratch),
        compiler_params=pltpu.CompilerParams(vmem_limit_bytes=limit),
        cost_estimate=pl.CostEstimate(flops=flops, bytes_accessed=moved, transcendentals=exps),
    )


def moved_block(seg, flags, blocks, cap):
    out = jnp.int32(blocks)
    for b in range(blocks):
        out = jnp.where(flags[0, seg[0, b * cap]] == 1, jnp.int32(b), out)
    return out


def attend(segment_ids, move_flags, queries, key_rows, value_rows, out_cotangent):
    home, width = queries.shape
    dest, part = out_cotangent.shape
    cap = dest - home
    return call(
        functools.partial(forward_kernel, cap),
        [
            ((1,), jnp.int32),
            ((cap, part), BF16),
            ((dest, width), BF16),
            ((cap, width), BF16),
            ((width // HEAD, home, home), BF16),
        ],
        [SMEM, SMEM] + [VMEM] * 4,
        [pltpu.VMEM((home // cap + 1, cap, width), BF16)],
    )(segment_ids, move_flags, queries, key_rows, value_rows, out_cotangent)


def forward_kernel(cap, seg, flags, q, k, v, cot, gone_out, picked, att, sent, pt, rows_buf):
    rows, width = q.shape
    blocks = rows // cap
    gone = moved_block(seg, flags, blocks, cap)
    gone_out[0] = gone
    row = jnp.where(gone == blocks, blocks, blocks - 1)
    picked[...] = cot[pl.ds(pl.multiple_of(row * cap, cap), cap), :]
    col_block = lax.broadcasted_iota(jnp.int32, (rows, 1), 0) // cap
    row_block = lax.broadcasted_iota(jnp.int32, (1, rows), 1) // cap
    key_id = jnp.zeros((rows, 1), jnp.int32)
    query_id = jnp.zeros((1, rows), jnp.int32)
    for b in range(blocks):
        image = seg[0, b * cap]
        key_id = jnp.where(col_block == b, image, key_id)
        query_id = jnp.where(row_block == b, image, query_id)
    same = key_id == query_id
    for h in range(width // HEAD):
        cols = slice(h * HEAD, (h + 1) * HEAD)
        scores = nt(k[:, cols], q[:, cols]) * HEAD ** (-0.5)
        scores = jnp.where(same, scores, -1e30)
        weights = jnp.exp(scores - jnp.max(scores, axis=0, keepdims=True))
        weights = weights * (1.0 / jnp.sum(weights, axis=0, keepdims=True))
        weights = weights.astype(BF16)
        pt[h] = weights
        out = tn(weights, v[:, cols]).astype(BF16)
        for b in range(blocks):
            slot = jnp.where(b < gone, b, jnp.where(b == gone, blocks, b - 1))
            rows_buf[slot, :, cols] = out[b * cap : (b + 1) * cap]
    empty = jnp.where(gone == blocks, blocks, blocks - 1)
    rows_buf[empty] = jnp.zeros((cap, width), BF16)
    for b in range(blocks):
        att[b * cap : (b + 1) * cap] = rows_buf[b]
    att[rows:] = jnp.zeros((cap, width), BF16)
    sent[...] = rows_buf[blocks]


def share_kernel(part, cols, t, place, weight, *refs):
    outs, direct, sems = refs[:-2], refs[-2], refs[-1]
    rest = direct.shape[1] // 2
    far = (1 - (t[0] >> 1)) * 2 * part
    at = far + (place[0] >> 1) * part + (place[0] & 1) * cols
    moves = []
    for out in outs:
        moves.append((at, out))
        at += out.shape[1]
    for k in range(2):
        moves.append((far + (k + 1) * part - rest, direct.at[:, pl.ds(k * rest, rest)]))
    copies = []
    for i, (start, out) in enumerate(moves):
        where = pl.ds(pl.multiple_of(start, HEAD), out.shape[1])
        copies.append(pltpu.make_async_copy(weight.at[:, where], out, sems.at[i]))
    for c in copies:
        c.start()
    for c in copies:
        c.wait()


def home_kernel(cap, blocks, gone_ref, *refs):
    gone = gone_ref[0]
    n = len(refs) // 3
    cots, backs, outs = refs[:n], refs[n : 2 * n], refs[2 * n :]
    for cot, out in zip(cots, outs):
        for b in range(blocks):
            start = pl.multiple_of((b - (b > gone).astype(jnp.int32)) * cap, cap)
            out[b * cap : (b + 1) * cap] = cot[pl.ds(start, cap), :]

    @pl.when(gone < blocks)
    def _():
        for back, out in zip(backs, outs):
            out[pl.ds(pl.multiple_of(gone * cap, cap), cap), :] = back[...]


def own_kernel(t_ref, cot_own, cot_sib, weight, out):
    part = cot_own.shape[1]
    t = t_ref[0]
    total = None
    for cot, i in ((cot_own, t), (cot_sib, t ^ 1)):
        start = pl.multiple_of(i * part, part)
        term = nt(cot[...], weight[:, pl.ds(start, part)])
        total = term if total is None else total + term
    out[...] = total


def by_place(t, place, own, sib, run):
    same = (t & 1) == (place >> 1)
    pl.when(same)(lambda: run(own, sib))
    pl.when(jnp.logical_not(same))(lambda: run(sib, own))


def far_kernel(t, place, cot_own, cot_sib, *refs):
    out, chunks = refs[-1], refs[:-1]
    chunks = [chunks[i : i + 3] for i in range(0, len(chunks), 3)]
    cols = sum(c[0].shape[1] for c in chunks)
    y = place[0] & 1

    def run(a, b):
        total = None
        at = 0
        for mine, by_y, by_z in chunks:
            size = mine.shape[1]
            near_at = pl.ds(pl.multiple_of(y * cols + at, HEAD), size)
            next_at = pl.ds(pl.multiple_of((1 - y) * cols + at, HEAD), size)
            term = nt(a[:, near_at], mine[...]) + nt(a[:, next_at], by_y[...])
            term += nt(b[:, near_at], by_z[...])
            total = term if total is None else total + term
            at += size
        out[...] = total

    by_place(t[0], place[0], cot_own, cot_sib, run)


def last_kernel(t, place, cot_own, cot_sib, part_sum, diag_a, diag_b, direct, out):
    cols = diag_a.shape[1]
    rest = direct.shape[1] // 2
    core = t[0] & 1
    at = pl.ds(pl.multiple_of((1 - (place[0] & 1)) * cols, HEAD), cols)
    own_at = pl.ds(pl.multiple_of(core * rest, HEAD), rest)
    sib_at = pl.ds(pl.multiple_of((1 - core) * rest, HEAD), rest)

    def run(a, b):
        diag = jnp.concatenate([diag_a[...], diag_b[...]], axis=0)
        total = part_sum[...] + nt(b[:, at], diag)
        total += nt(cot_own[:, 2 * cols :], direct[:, own_at])
        total += nt(cot_sib[:, 2 * cols :], direct[:, sib_at])
        out[...] = total.astype(BF16)

    by_place(t[0], place[0], cot_own, cot_sib, run)


def fill_left(cap, gone, att, far_att, left):
    rows, width = att.shape
    last = rows - 2 * cap
    swap = gone * cap < rows - cap
    for i, src in enumerate((att, far_att)):
        where = slice(i * width, (i + 1) * width)
        left[:last, where] = src[:last]
        home, came = src[last : rows - cap, :], src[rows - cap :, :]
        left[last : rows - cap, where] = jnp.where(swap, came, home)
        left[rows - cap :, where] = jnp.where(swap, home, came)


def early_kernel(cap, part, gone, t_ref, place_ref, att, far_att, weight, *refs):
    own_out, sib_out, left = refs[-3:]
    chunks = [refs[i : i + 3] for i in range(0, len(refs) - 3, 3)]
    t, place = t_ref[0], place_ref[0]
    y, z = place & 1, place >> 1
    cols = own_out.shape[1] // 2
    fill_left(cap, gone[0], att, far_att, left)

    def run(a, b):
        at = 0
        for mine, by_y, by_z in chunks:
            size = mine.shape[1]
            for out, k, j, far_weight in (
                (a, z, y, mine),
                (a, z, 1 - y, by_y),
                (b, 1 - z, y, by_z),
            ):
                start = pl.multiple_of(((t >> 1) * 2 + k) * part + j * cols + at, HEAD)
                both = jnp.concatenate([weight[:, pl.ds(start, size)], far_weight[...]], axis=0)
                here = pl.ds(pl.multiple_of(j * cols + at, HEAD), size)
                out[:, here] = nn(left[...], both).astype(BF16)
            at += size

    by_place(t, place, own_out, sib_out, run)


def late_kernel(t_ref, place_ref, left, weight, diag_a, diag_b, direct, own_out, sib_out):
    t, place = t_ref[0], place_ref[0]
    core, y, z = t & 1, place & 1, place >> 1
    part = weight.shape[1] // 4
    cols = diag_a.shape[1]
    rest = direct.shape[1] // 2

    def product(k, at, size, *far_weight):
        start = pl.multiple_of(((t >> 1) * 2 + k) * part + at, HEAD)
        both = jnp.concatenate([weight[:, pl.ds(start, size)], *far_weight], axis=0)
        return nn(left[...], both).astype(BF16)

    value = product(1 - z, (1 - y) * cols, cols, diag_a[...], diag_b[...])
    own_out[:, :cols] = value
    sib_out[:, :cols] = value
    for out, k in ((own_out, core), (sib_out, 1 - core)):
        where = pl.ds(pl.multiple_of(k * rest, HEAD), rest)
        out[:, cols:] = product(k, 2 * cols, rest, direct[:, where])


def join_kernel(cap, t_ref, place_ref, own, other, own_late, other_late, out, buf, sems):
    t, place = t_ref[0], place_ref[0]
    y, z = place & 1, place >> 1
    cols = own.shape[1] // 2
    same = (t & 1) == z

    def add(a, b):
        return (a.astype(F32) + b.astype(F32)).astype(BF16)

    copies = []
    for i in range(own.shape[0] // cap):
        rows = slice(i * cap, (i + 1) * cap)

        @pl.when(same)
        def _(rows=rows):
            buf[rows, : 2 * cols] = add(own[rows], other[rows])

        @pl.when(jnp.logical_not(same))
        def _(rows=rows):
            here = pl.ds(pl.multiple_of(y * cols, HEAD), cols)
            buf[rows, here] = add(own[rows, here], other[rows, here])
            there = pl.ds(pl.multiple_of((1 - y) * cols, HEAD), cols)
            buf[rows, there] = add(own_late[rows, :cols], other_late[rows, :cols])

        buf[rows, 2 * cols :] = add(own_late[rows, cols:], other_late[rows, cols:])
        where = pl.ds(i * cap, cap)
        copy = pltpu.make_async_copy(buf.at[where, :], out.at[where, :], sems.at[i])
        copy.start()
        copies.append(copy)
    for copy in copies:
        copy.wait()


def backward_kernel(q, k, v, pt, near, far, gq, gk, gv, bq, bk, bv, sems):
    copies = []
    for h in range(q.shape[1] // HEAD):
        cols = slice(h * HEAD, (h + 1) * HEAD)
        where = pl.ds(h * HEAD, HEAD)

        def send(buf, out, n, where=where, h=h):
            copy = pltpu.make_async_copy(buf.at[:, where], out.at[:, where], sems.at[3 * h + n])
            copy.start()
            copies.append(copy)

        cot = (near[:, cols] + far[:, cols].astype(F32)).astype(BF16)
        weights = pt[h]
        bv[:, cols] = nn(weights, cot).astype(BF16)
        send(bv, gv, 0)
        rise = nt(v[:, cols], cot)
        wide = weights.astype(F32)
        mean = jnp.sum(wide * rise, axis=0, keepdims=True)
        slope = (wide * (rise - mean) * HEAD ** (-0.5)).astype(BF16)
        bk[:, cols] = nn(slope, q[:, cols]).astype(BF16)
        send(bk, gk, 1)
        bq[:, cols] = tn(slope, k[:, cols]).astype(BF16)
        send(bq, gq, 2)
    for copy in copies:
        copy.wait()


def gradients(queries, key_rows, value_rows, pt, near, far, flops):
    home, width = queries.shape
    return call(
        backward_kernel,
        [((home, width), BF16)] * 3,
        [VMEM] * 6,
        [pltpu.VMEM((home, width), BF16)] * 3
        + [pltpu.SemaphoreType.DMA((3 * (width // HEAD),))],
        flops=flops,
        moved=9 * home * width * 2,
        out=ANY,
    )(queries, key_rows, value_rows, pt, near, far)


def flip(values, axis, by):
    size = lax.axis_size(axis)
    return lax.ppermute(values, axis, [(i, i ^ by) for i in range(size)])


def shifted(values, axis, by):
    size = lax.axis_size(axis)
    return lax.ppermute(values, axis, [(i, (i + by) % size) for i in range(size)])


def tie(value, *others):
    return lax.optimization_barrier((value, *others))[0]


def shards(queries, key_rows, value_rows, out_weight, segment_ids, move_flags, out_cotangent):
    home, width = queries.shape
    dest, part = out_cotangent.shape
    cap = dest - home
    blocks = home // cap
    heads = width // HEAD
    cols = part * 5 // 12 // HEAD * HEAD
    rest = part - 2 * cols
    t = lax.axis_index("tensor").astype(jnp.int32).reshape(1)
    place = (lax.axis_index("dp").astype(jnp.int32) & 3).reshape(1)

    share, direct = call(
        functools.partial(share_kernel, part, cols),
        [((width, cols), BF16), ((width, 2 * rest), BF16)],
        [SMEM, SMEM, ANY],
        [pltpu.SemaphoreType.DMA((3,))],
        limit=OPEN_LIMIT,
    )(t, place, out_weight)
    first = flip(share, "tensor", 2)
    cot_raw = flip(out_cotangent, "tensor", 1)

    gone, picked, att, sent, pt = attend(
        tie(segment_ids, share), move_flags, queries, key_rows, value_rows, out_cotangent
    )
    back = shifted(picked, "dp", -1)
    came = shifted(sent, "dp", 1)

    first, back, came = lax.optimization_barrier((first, back, came))
    by_y = flip(first, "dp", 1)
    by_z = flip(first, "dp", 2)
    att = lax.dynamic_update_slice(att, came, (home, 0))
    far_att = flip(att, "tensor", 2)
    direct = flip(tie(direct, att), "tensor", 2)
    back_sib = flip(back, "tensor", 1)

    cot_own, cot_sib = call(
        functools.partial(home_kernel, cap, blocks),
        [((home, part), BF16)] * 2,
        [SMEM] + [VMEM] * 4,
    )(gone, out_cotangent, cot_raw, back, back_sib)

    near = call(
        own_kernel,
        [((home, width), F32)],
        [SMEM, VMEM, VMEM, VMEM],
        flops=4 * home * width * part,
        moved=(home + width) * part * 4,
    )(t, cot_own, cot_sib, out_weight)[0]

    by_y, by_z, near, far_att = lax.optimization_barrier((by_y, by_z, near, far_att))
    rows_a = width * 7 // 12 // 32 * 32
    diag_a = flip(by_y[:rows_a], "dp", 2)
    diag_b = flip(by_z[rows_a:], "dp", 1)

    early = (first, by_y, by_z)
    half = call(
        far_kernel,
        [((home, width), F32)],
        [SMEM, SMEM] + [VMEM] * 5,
        flops=6 * home * width * cols,
        moved=(home + width) * cols * 6,
    )(t, place, cot_own, cot_sib, *early)[0]
    send = call(
        last_kernel,
        [((home, width), BF16)],
        [SMEM, SMEM] + [VMEM] * 6,
        flops=2 * home * width * (cols + 2 * rest),
        moved=(home + width) * (cols + 2 * rest) * 2,
    )(t, place, cot_own, cot_sib, half, diag_a, diag_b, direct)[0]
    far = flip(send, "tensor", 2)
    own, sib, left = call(
        functools.partial(early_kernel, cap, part),
        [((dest, 2 * cols), BF16), ((dest, 2 * cols), BF16), ((dest, 2 * width), BF16)],
        [SMEM] * 3 + [VMEM] * 6,
        flops=12 * dest * width * cols,
        moved=12 * width * cols + dest * part * 4,
    )(gone, t, tie(place, send), att, far_att, out_weight, *early)
    other = flip(sib, "tensor", 1)
    own_late, sib_late = call(
        late_kernel,
        [((dest, cols + rest), BF16)] * 2,
        [SMEM] * 2 + [VMEM] * 5,
        flops=4 * dest * width * (cols + 2 * rest),
        moved=4 * width * (cols + 2 * rest) + dest * part * 2,
    )(t, tie(place, send), left, out_weight, diag_a, diag_b, direct)
    other_late = flip(sib_late, "tensor", 1)
    projected = call(
        functools.partial(join_kernel, cap),
        [((dest, part), BF16)],
        [SMEM] * 2 + [VMEM] * 4,
        [pltpu.VMEM((dest, part), BF16), pltpu.SemaphoreType.DMA((blocks + 1,))],
        moved=dest * part * 6,
        out=ANY,
    )(t, place, own, other, own_late, other_late)[0]

    grad_q, grad_k, grad_v = gradients(
        queries, key_rows, value_rows, pt, near, far, 800 * home * home * width
    )
    return (projected, grad_q, grad_k, grad_v)


def wide_shards(queries, key_rows, value_rows, out_weight, segment_ids, move_flags, out_cotangent):
    home, width = queries.shape
    dest, part = out_cotangent.shape
    cap = dest - home
    blocks = home // cap
    heads = width // HEAD
    gone, picked, att, sent, pt = attend(
        segment_ids, move_flags, queries, key_rows, value_rows, out_cotangent
    )
    came = shifted(sent, "dp", 1)
    kept = jnp.where(gone[0] < blocks, home - cap, home)
    att = lax.dynamic_update_slice(att, came, (kept, 0))
    term = jnp.dot(att, out_weight, preferred_element_type=F32).astype(BF16)
    projected = lax.psum_scatter(term, "tensor", scatter_dimension=1, tiled=True)
    back = shifted(picked, "dp", -1)
    cot = call(
        functools.partial(home_kernel, cap, blocks),
        [((home, part), BF16)],
        [SMEM, VMEM, VMEM],
    )(gone, out_cotangent, back)[0]
    whole = lax.all_gather(cot, "tensor", axis=1, tiled=True)
    near = nt(whole, out_weight)
    none = jnp.zeros((home, width), BF16)
    grad_q, grad_k, grad_v = gradients(queries, key_rows, value_rows, pt, near, none, 0)
    return (projected, grad_q, grad_k, grad_v)


def solution(mesh):
    square = mesh.shape["tensor"] == 4 and mesh.shape["dp"] % 4 == 0
    in_specs = (
        P("dp", "tensor"),
        P("dp", "tensor"),
        P("dp", "tensor"),
        P("tensor", None),
        P("dp", None),
        P("dp", None),
        P("dp", "tensor"),
    )
    out_specs = (P("dp", "tensor"), P("dp", "tensor"), P("dp", "tensor"), P("dp", "tensor"))
    return jax.shard_map(
        shards if square else wide_shards,
        mesh=mesh,
        in_specs=in_specs,
        out_specs=out_specs,
        check_vma=False,
    )
```

```python
import functools

import jax
import jax.numpy as jnp
from jax import lax
from jax.experimental import pallas as pl
from jax.experimental.pallas import tpu as pltpu
from jax.sharding import PartitionSpec as P

HEAD = 128
BF16 = jnp.bfloat16
F32 = jnp.float32
VMEM = pl.BlockSpec(memory_space=pltpu.VMEM)
SMEM = pl.BlockSpec(memory_space=pltpu.SMEM)
ANY = pl.BlockSpec(memory_space=pl.ANY)
LIMIT = 16 * 1024 * 1024
OPEN_LIMIT = 52 * 1024 * 1024


def nt(a, b):
    return lax.dot_general(a, b, (((1,), (1,)), ((), ())), preferred_element_type=F32)


def nn(a, b):
    return lax.dot_general(a, b, (((1,), (0,)), ((), ())), preferred_element_type=F32)


def tn(a, b):
    return lax.dot_general(a, b, (((0,), (0,)), ((), ())), preferred_element_type=F32)


def call(kernel, outs, ins, scratch=(), flops=0, moved=0, exps=0, limit=LIMIT, out=None):
    return pl.pallas_call(
        kernel,
        out_shape=tuple(jax.ShapeDtypeStruct(s, t) for s, t in outs),
        in_specs=list(ins),
        out_specs=tuple(out or (SMEM if t == jnp.int32 else VMEM) for _, t in outs),
        scratch_shapes=list(scratch),
        compiler_params=pltpu.CompilerParams(vmem_limit_bytes=limit),
        cost_estimate=pl.CostEstimate(flops=flops, bytes_accessed=moved, transcendentals=exps),
    )


def moved_block(seg, flags, blocks, cap):
    out = jnp.int32(blocks)
    for b in range(blocks):
        out = jnp.where(flags[0, seg[0, b * cap]] == 1, jnp.int32(b), out)
    return out


def attend(segment_ids, move_flags, queries, key_rows, value_rows, out_cotangent):
    home, width = queries.shape
    dest, part = out_cotangent.shape
    cap = dest - home
    return call(
        functools.partial(forward_kernel, cap),
        [
            ((1,), jnp.int32),
            ((cap, part), BF16),
            ((dest, width), BF16),
            ((cap, width), BF16),
            ((width // HEAD, home, home), BF16),
        ],
        [SMEM, SMEM] + [VMEM] * 4,
        [pltpu.VMEM((home // cap + 1, cap, width), BF16)],
    )(segment_ids, move_flags, queries, key_rows, value_rows, out_cotangent)


def forward_kernel(cap, seg, flags, q, k, v, cot, gone_out, picked, att, sent, pt, rows_buf):
    rows, width = q.shape
    blocks = rows // cap
    gone = moved_block(seg, flags, blocks, cap)
    gone_out[0] = gone
    row = jnp.where(gone == blocks, blocks, blocks - 1)
    picked[...] = cot[pl.ds(pl.multiple_of(row * cap, cap), cap), :]
    col_block = lax.broadcasted_iota(jnp.int32, (rows, 1), 0) // cap
    row_block = lax.broadcasted_iota(jnp.int32, (1, rows), 1) // cap
    key_id = jnp.zeros((rows, 1), jnp.int32)
    query_id = jnp.zeros((1, rows), jnp.int32)
    for b in range(blocks):
        image = seg[0, b * cap]
        key_id = jnp.where(col_block == b, image, key_id)
        query_id = jnp.where(row_block == b, image, query_id)
    same = key_id == query_id
    for h in range(width // HEAD):
        cols = slice(h * HEAD, (h + 1) * HEAD)
        scores = nt(k[:, cols], q[:, cols]) * HEAD ** (-0.5)
        scores = jnp.where(same, scores, -1e30)
        weights = jnp.exp(scores - jnp.max(scores, axis=0, keepdims=True))
        weights = weights * (1.0 / jnp.sum(weights, axis=0, keepdims=True))
        weights = weights.astype(BF16)
        pt[h] = weights
        out = tn(weights, v[:, cols]).astype(BF16)
        for b in range(blocks):
            slot = jnp.where(b < gone, b, jnp.where(b == gone, blocks, b - 1))
            rows_buf[slot, :, cols] = out[b * cap : (b + 1) * cap]
    empty = jnp.where(gone == blocks, blocks, blocks - 1)
    rows_buf[empty] = jnp.zeros((cap, width), BF16)
    for b in range(blocks):
        att[b * cap : (b + 1) * cap] = rows_buf[b]
    att[rows:] = jnp.zeros((cap, width), BF16)
    sent[...] = rows_buf[blocks]


def share_kernel(part, cols, t, place, weight, *refs):
    outs, direct, sems = refs[:-2], refs[-2], refs[-1]
    rest = direct.shape[1] // 2
    far = (1 - (t[0] >> 1)) * 2 * part
    at = far + (place[0] >> 1) * part + (place[0] & 1) * cols
    moves = []
    for out in outs:
        moves.append((at, out))
        at += out.shape[1]
    for k in range(2):
        moves.append((far + (k + 1) * part - rest, direct.at[:, pl.ds(k * rest, rest)]))
    copies = []
    for i, (start, out) in enumerate(moves):
        where = pl.ds(pl.multiple_of(start, HEAD), out.shape[1])
        copies.append(pltpu.make_async_copy(weight.at[:, where], out, sems.at[i]))
    for c in copies:
        c.start()
    for c in copies:
        c.wait()


def home_kernel(cap, blocks, gone_ref, *refs):
    gone = gone_ref[0]
    n = len(refs) // 3
    cots, backs, outs = refs[:n], refs[n : 2 * n], refs[2 * n :]
    for cot, out in zip(cots, outs):
        for b in range(blocks):
            start = pl.multiple_of((b - (b > gone).astype(jnp.int32)) * cap, cap)
            out[b * cap : (b + 1) * cap] = cot[pl.ds(start, cap), :]

    @pl.when(gone < blocks)
    def _():
        for back, out in zip(backs, outs):
            out[pl.ds(pl.multiple_of(gone * cap, cap), cap), :] = back[...]


def own_kernel(t_ref, cot_own, cot_sib, weight, out):
    part = cot_own.shape[1]
    t = t_ref[0]
    total = None
    for cot, i in ((cot_own, t), (cot_sib, t ^ 1)):
        start = pl.multiple_of(i * part, part)
        term = nt(cot[...], weight[:, pl.ds(start, part)])
        total = term if total is None else total + term
    out[...] = total


def by_place(t, place, own, sib, run):
    same = (t & 1) == (place >> 1)
    pl.when(same)(lambda: run(own, sib))
    pl.when(jnp.logical_not(same))(lambda: run(sib, own))


def far_kernel(t, place, cot_own, cot_sib, *refs):
    out, chunks = refs[-1], refs[:-1]
    chunks = [chunks[i : i + 3] for i in range(0, len(chunks), 3)]
    cols = sum(c[0].shape[1] for c in chunks)
    y = place[0] & 1

    def run(a, b):
        total = None
        at = 0
        for mine, by_y, by_z in chunks:
            size = mine.shape[1]
            near_at = pl.ds(pl.multiple_of(y * cols + at, HEAD), size)
            next_at = pl.ds(pl.multiple_of((1 - y) * cols + at, HEAD), size)
            term = nt(a[:, near_at], mine[...]) + nt(a[:, next_at], by_y[...])
            term += nt(b[:, near_at], by_z[...])
            total = term if total is None else total + term
            at += size
        out[...] = total

    by_place(t[0], place[0], cot_own, cot_sib, run)


def last_kernel(t, place, cot_own, cot_sib, part_sum, diag_a, diag_b, direct, out):
    cols = diag_a.shape[1]
    rest = direct.shape[1] // 2
    core = t[0] & 1
    at = pl.ds(pl.multiple_of((1 - (place[0] & 1)) * cols, HEAD), cols)
    own_at = pl.ds(pl.multiple_of(core * rest, HEAD), rest)
    sib_at = pl.ds(pl.multiple_of((1 - core) * rest, HEAD), rest)

    def run(a, b):
        diag = jnp.concatenate([diag_a[...], diag_b[...]], axis=0)
        total = part_sum[...] + nt(b[:, at], diag)
        total += nt(cot_own[:, 2 * cols :], direct[:, own_at])
        total += nt(cot_sib[:, 2 * cols :], direct[:, sib_at])
        out[...] = total.astype(BF16)

    by_place(t[0], place[0], cot_own, cot_sib, run)


def fill_left(cap, gone, att, far_att, left):
    rows, width = att.shape
    last = rows - 2 * cap
    swap = gone * cap < rows - cap
    for i, src in enumerate((att, far_att)):
        where = slice(i * width, (i + 1) * width)
        left[:last, where] = src[:last]
        home, came = src[last : rows - cap, :], src[rows - cap :, :]
        left[last : rows - cap, where] = jnp.where(swap, came, home)
        left[rows - cap :, where] = jnp.where(swap, home, came)


def early_kernel(cap, part, gone, t_ref, place_ref, att, far_att, weight, *refs):
    own_out, sib_out, left = refs[-3:]
    chunks = [refs[i : i + 3] for i in range(0, len(refs) - 3, 3)]
    t, place = t_ref[0], place_ref[0]
    y, z = place & 1, place >> 1
    cols = own_out.shape[1] // 2
    fill_left(cap, gone[0], att, far_att, left)

    def run(a, b):
        at = 0
        for mine, by_y, by_z in chunks:
            size = mine.shape[1]
            for out, k, j, far_weight in (
                (a, z, y, mine),
                (a, z, 1 - y, by_y),
                (b, 1 - z, y, by_z),
            ):
                start = pl.multiple_of(((t >> 1) * 2 + k) * part + j * cols + at, HEAD)
                both = jnp.concatenate([weight[:, pl.ds(start, size)], far_weight[...]], axis=0)
                here = pl.ds(pl.multiple_of(j * cols + at, HEAD), size)
                out[:, here] = nn(left[...], both).astype(BF16)
            at += size

    by_place(t, place, own_out, sib_out, run)


def late_kernel(t_ref, place_ref, left, weight, diag_a, diag_b, direct, own_out, sib_out):
    t, place = t_ref[0], place_ref[0]
    core, y, z = t & 1, place & 1, place >> 1
    part = weight.shape[1] // 4
    cols = diag_a.shape[1]
    rest = direct.shape[1] // 2

    def product(k, at, size, *far_weight):
        start = pl.multiple_of(((t >> 1) * 2 + k) * part + at, HEAD)
        both = jnp.concatenate([weight[:, pl.ds(start, size)], *far_weight], axis=0)
        return nn(left[...], both).astype(BF16)

    value = product(1 - z, (1 - y) * cols, cols, diag_a[...], diag_b[...])
    own_out[:, :cols] = value
    sib_out[:, :cols] = value
    for out, k in ((own_out, core), (sib_out, 1 - core)):
        where = pl.ds(pl.multiple_of(k * rest, HEAD), rest)
        out[:, cols:] = product(k, 2 * cols, rest, direct[:, where])


def join_kernel(cap, t_ref, place_ref, own, other, own_late, other_late, out, buf, sems):
    t, place = t_ref[0], place_ref[0]
    y, z = place & 1, place >> 1
    cols = own.shape[1] // 2
    same = (t & 1) == z

    def add(a, b):
        return (a.astype(F32) + b.astype(F32)).astype(BF16)

    copies = []
    for i in range(own.shape[0] // cap):
        rows = slice(i * cap, (i + 1) * cap)

        @pl.when(same)
        def _(rows=rows):
            buf[rows, : 2 * cols] = add(own[rows], other[rows])

        @pl.when(jnp.logical_not(same))
        def _(rows=rows):
            here = pl.ds(pl.multiple_of(y * cols, HEAD), cols)
            buf[rows, here] = add(own[rows, here], other[rows, here])
            there = pl.ds(pl.multiple_of((1 - y) * cols, HEAD), cols)
            buf[rows, there] = add(own_late[rows, :cols], other_late[rows, :cols])

        buf[rows, 2 * cols :] = add(own_late[rows, cols:], other_late[rows, cols:])
        where = pl.ds(i * cap, cap)
        copy = pltpu.make_async_copy(buf.at[where, :], out.at[where, :], sems.at[i])
        copy.start()
        copies.append(copy)
    for copy in copies:
        copy.wait()


def backward_kernel(q, k, v, pt, near, far, gq, gk, gv, bq, bk, bv, sems):
    copies = []
    for h in range(q.shape[1] // HEAD):
        cols = slice(h * HEAD, (h + 1) * HEAD)
        where = pl.ds(h * HEAD, HEAD)

        def send(buf, out, n, where=where, h=h):
            copy = pltpu.make_async_copy(buf.at[:, where], out.at[:, where], sems.at[3 * h + n])
            copy.start()
            copies.append(copy)

        cot = (near[:, cols] + far[:, cols].astype(F32)).astype(BF16)
        weights = pt[h]
        bv[:, cols] = nn(weights, cot).astype(BF16)
        send(bv, gv, 0)
        rise = nt(v[:, cols], cot)
        wide = weights.astype(F32)
        mean = jnp.sum(wide * rise, axis=0, keepdims=True)
        slope = (wide * (rise - mean) * HEAD ** (-0.5)).astype(BF16)
        bk[:, cols] = nn(slope, q[:, cols]).astype(BF16)
        send(bk, gk, 1)
        bq[:, cols] = tn(slope, k[:, cols]).astype(BF16)
        send(bq, gq, 2)
    for copy in copies:
        copy.wait()


def gradients(queries, key_rows, value_rows, pt, near, far, flops):
    home, width = queries.shape
    return call(
        backward_kernel,
        [((home, width), BF16)] * 3,
        [VMEM] * 6,
        [pltpu.VMEM((home, width), BF16)] * 3
        + [pltpu.SemaphoreType.DMA((3 * (width // HEAD),))],
        flops=flops,
        moved=9 * home * width * 2,
        out=ANY,
    )(queries, key_rows, value_rows, pt, near, far)


def flip(values, axis, by):
    size = lax.axis_size(axis)
    return lax.ppermute(values, axis, [(i, i ^ by) for i in range(size)])


def shifted(values, axis, by):
    size = lax.axis_size(axis)
    return lax.ppermute(values, axis, [(i, (i + by) % size) for i in range(size)])


def tie(value, *others):
    return lax.optimization_barrier((value, *others))[0]


def shards(queries, key_rows, value_rows, out_weight, segment_ids, move_flags, out_cotangent):
    home, width = queries.shape
    dest, part = out_cotangent.shape
    cap = dest - home
    blocks = home // cap
    heads = width // HEAD
    cols = part * 5 // 12 // HEAD * HEAD
    rest = part - 2 * cols
    t = lax.axis_index("tensor").astype(jnp.int32).reshape(1)
    place = (lax.axis_index("dp").astype(jnp.int32) & 3).reshape(1)

    share, direct = call(
        functools.partial(share_kernel, part, cols),
        [((width, cols), BF16), ((width, 2 * rest), BF16)],
        [SMEM, SMEM, ANY],
        [pltpu.SemaphoreType.DMA((3,))],
        limit=OPEN_LIMIT,
    )(t, place, out_weight)
    first = flip(share, "tensor", 2)
    cot_raw = flip(out_cotangent, "tensor", 1)

    gone, picked, att, sent, pt = attend(
        tie(segment_ids, share), move_flags, queries, key_rows, value_rows, out_cotangent
    )
    back = shifted(picked, "dp", -1)
    came = shifted(sent, "dp", 1)

    first, back, came = lax.optimization_barrier((first, back, came))
    by_y = flip(first, "dp", 1)
    by_z = flip(first, "dp", 2)
    att = lax.dynamic_update_slice(att, came, (home, 0))
    far_att = flip(att, "tensor", 2)
    direct = flip(tie(direct, att), "tensor", 2)
    back_sib = flip(back, "tensor", 1)

    cot_own, cot_sib = call(
        functools.partial(home_kernel, cap, blocks),
        [((home, part), BF16)] * 2,
        [SMEM] + [VMEM] * 4,
    )(gone, out_cotangent, cot_raw, back, back_sib)

    near = call(
        own_kernel,
        [((home, width), F32)],
        [SMEM, VMEM, VMEM, VMEM],
        flops=4 * home * width * part,
        moved=(home + width) * part * 4,
    )(t, cot_own, cot_sib, out_weight)[0]

    by_y, near, far_att = lax.optimization_barrier((by_y, near, far_att))
    by_z = tie(by_z, near)
    rows_a = width * 7 // 12 // 32 * 32
    diag_a = flip(by_y[:rows_a], "dp", 2)
    diag_b = flip(by_z[rows_a:], "dp", 1)

    early = (first, by_y, by_z)
    half = call(
        far_kernel,
        [((home, width), F32)],
        [SMEM, SMEM] + [VMEM] * 5,
        flops=6 * home * width * cols,
        moved=(home + width) * cols * 6,
    )(t, place, cot_own, cot_sib, *early)[0]
    send = call(
        last_kernel,
        [((home, width), BF16)],
        [SMEM, SMEM] + [VMEM] * 6,
        flops=2 * home * width * (cols + 2 * rest),
        moved=(home + width) * (cols + 2 * rest) * 2,
    )(t, place, cot_own, cot_sib, half, diag_a, diag_b, direct)[0]
    far = flip(send, "tensor", 2)
    own, sib, left = call(
        functools.partial(early_kernel, cap, part),
        [((dest, 2 * cols), BF16), ((dest, 2 * cols), BF16), ((dest, 2 * width), BF16)],
        [SMEM] * 3 + [VMEM] * 6,
        flops=12 * dest * width * cols,
        moved=12 * width * cols + dest * part * 4,
    )(gone, t, tie(place, send), att, far_att, out_weight, *early)
    other = flip(sib, "tensor", 1)
    own_late, sib_late = call(
        late_kernel,
        [((dest, cols + rest), BF16)] * 2,
        [SMEM] * 2 + [VMEM] * 5,
        flops=4 * dest * width * (cols + 2 * rest),
        moved=4 * width * (cols + 2 * rest) + dest * part * 2,
    )(t, tie(place, send), left, out_weight, diag_a, diag_b, direct)
    other_late = flip(sib_late, "tensor", 1)
    projected = call(
        functools.partial(join_kernel, cap),
        [((dest, part), BF16)],
        [SMEM] * 2 + [VMEM] * 4,
        [pltpu.VMEM((dest, part), BF16), pltpu.SemaphoreType.DMA((blocks + 1,))],
        moved=dest * part * 6,
        out=ANY,
    )(t, place, own, other, own_late, other_late)[0]

    grad_q, grad_k, grad_v = gradients(
        queries, key_rows, value_rows, pt, near, far, 800 * home * home * width
    )
    return (projected, grad_q, grad_k, grad_v)


def wide_shards(queries, key_rows, value_rows, out_weight, segment_ids, move_flags, out_cotangent):
    home, width = queries.shape
    dest, part = out_cotangent.shape
    cap = dest - home
    blocks = home // cap
    heads = width // HEAD
    gone, picked, att, sent, pt = attend(
        segment_ids, move_flags, queries, key_rows, value_rows, out_cotangent
    )
    came = shifted(sent, "dp", 1)
    kept = jnp.where(gone[0] < blocks, home - cap, home)
    att = lax.dynamic_update_slice(att, came, (kept, 0))
    term = jnp.dot(att, out_weight, preferred_element_type=F32).astype(BF16)
    projected = lax.psum_scatter(term, "tensor", scatter_dimension=1, tiled=True)
    back = shifted(picked, "dp", -1)
    cot = call(
        functools.partial(home_kernel, cap, blocks),
        [((home, part), BF16)],
        [SMEM, VMEM, VMEM],
    )(gone, out_cotangent, back)[0]
    whole = lax.all_gather(cot, "tensor", axis=1, tiled=True)
    near = nt(whole, out_weight)
    none = jnp.zeros((home, width), BF16)
    grad_q, grad_k, grad_v = gradients(queries, key_rows, value_rows, pt, near, none, 0)
    return (projected, grad_q, grad_k, grad_v)


def solution(mesh):
    square = mesh.shape["tensor"] == 4 and mesh.shape["dp"] % 4 == 0
    in_specs = (
        P("dp", "tensor"),
        P("dp", "tensor"),
        P("dp", "tensor"),
        P("tensor", None),
        P("dp", None),
        P("dp", None),
        P("dp", "tensor"),
    )
    out_specs = (P("dp", "tensor"), P("dp", "tensor"), P("dp", "tensor"), P("dp", "tensor"))
    return jax.shard_map(
        shards if square else wide_shards,
        mesh=mesh,
        in_specs=in_specs,
        out_specs=out_specs,
        check_vma=False,
    )
```

```python
import functools

import jax
import jax.numpy as jnp
from jax import lax
from jax.experimental import pallas as pl
from jax.experimental.pallas import tpu as pltpu
from jax.sharding import PartitionSpec as P

HEAD = 128
BF16 = jnp.bfloat16
F32 = jnp.float32
VMEM = pl.BlockSpec(memory_space=pltpu.VMEM)
SMEM = pl.BlockSpec(memory_space=pltpu.SMEM)
ANY = pl.BlockSpec(memory_space=pl.ANY)
LIMIT = 16 * 1024 * 1024
OPEN_LIMIT = 52 * 1024 * 1024


def nt(a, b):
    return lax.dot_general(a, b, (((1,), (1,)), ((), ())), preferred_element_type=F32)


def nn(a, b):
    return lax.dot_general(a, b, (((1,), (0,)), ((), ())), preferred_element_type=F32)


def tn(a, b):
    return lax.dot_general(a, b, (((0,), (0,)), ((), ())), preferred_element_type=F32)


def call(kernel, outs, ins, scratch=(), flops=0, moved=0, exps=0, limit=LIMIT, out=None):
    return pl.pallas_call(
        kernel,
        out_shape=tuple(jax.ShapeDtypeStruct(s, t) for s, t in outs),
        in_specs=list(ins),
        out_specs=tuple(out or (SMEM if t == jnp.int32 else VMEM) for _, t in outs),
        scratch_shapes=list(scratch),
        compiler_params=pltpu.CompilerParams(vmem_limit_bytes=limit),
        cost_estimate=pl.CostEstimate(flops=flops, bytes_accessed=moved, transcendentals=exps),
    )


def moved_block(seg, flags, blocks, cap):
    out = jnp.int32(blocks)
    for b in range(blocks):
        out = jnp.where(flags[0, seg[0, b * cap]] == 1, jnp.int32(b), out)
    return out


def attend(segment_ids, move_flags, queries, key_rows, value_rows, out_cotangent):
    home, width = queries.shape
    dest, part = out_cotangent.shape
    cap = dest - home
    return call(
        functools.partial(forward_kernel, cap),
        [
            ((1,), jnp.int32),
            ((cap, part), BF16),
            ((dest, width), BF16),
            ((cap, width), BF16),
            ((width // HEAD, home, home), BF16),
        ],
        [SMEM, SMEM] + [VMEM] * 4,
        [pltpu.VMEM((home // cap + 1, cap, width), BF16)],
    )(segment_ids, move_flags, queries, key_rows, value_rows, out_cotangent)


def forward_kernel(cap, seg, flags, q, k, v, cot, gone_out, picked, att, sent, pt, rows_buf):
    rows, width = q.shape
    blocks = rows // cap
    gone = moved_block(seg, flags, blocks, cap)
    gone_out[0] = gone
    row = jnp.where(gone == blocks, blocks, blocks - 1)
    picked[...] = cot[pl.ds(pl.multiple_of(row * cap, cap), cap), :]
    col_block = lax.broadcasted_iota(jnp.int32, (rows, 1), 0) // cap
    row_block = lax.broadcasted_iota(jnp.int32, (1, rows), 1) // cap
    key_id = jnp.zeros((rows, 1), jnp.int32)
    query_id = jnp.zeros((1, rows), jnp.int32)
    for b in range(blocks):
        image = seg[0, b * cap]
        key_id = jnp.where(col_block == b, image, key_id)
        query_id = jnp.where(row_block == b, image, query_id)
    same = key_id == query_id
    for h in range(width // HEAD):
        cols = slice(h * HEAD, (h + 1) * HEAD)
        scores = nt(k[:, cols], q[:, cols]) * HEAD ** (-0.5)
        scores = jnp.where(same, scores, -1e30)
        weights = jnp.exp(scores - jnp.max(scores, axis=0, keepdims=True))
        weights = weights * (1.0 / jnp.sum(weights, axis=0, keepdims=True))
        weights = weights.astype(BF16)
        pt[h] = weights
        out = tn(weights, v[:, cols]).astype(BF16)
        for b in range(blocks):
            slot = jnp.where(b < gone, b, jnp.where(b == gone, blocks, b - 1))
            rows_buf[slot, :, cols] = out[b * cap : (b + 1) * cap]
    empty = jnp.where(gone == blocks, blocks, blocks - 1)
    rows_buf[empty] = jnp.zeros((cap, width), BF16)
    for b in range(blocks):
        att[b * cap : (b + 1) * cap] = rows_buf[b]
    att[rows:] = jnp.zeros((cap, width), BF16)
    sent[...] = rows_buf[blocks]


def share_kernel(part, cols, t, place, weight, *refs):
    outs, direct, sems = refs[:-2], refs[-2], refs[-1]
    rest = direct.shape[1] // 2
    far = (1 - (t[0] >> 1)) * 2 * part
    at = far + (place[0] >> 1) * part + (place[0] & 1) * cols
    moves = []
    for out in outs:
        moves.append((at, out))
        at += out.shape[1]
    for k in range(2):
        moves.append((far + (k + 1) * part - rest, direct.at[:, pl.ds(k * rest, rest)]))
    copies = []
    for i, (start, out) in enumerate(moves):
        where = pl.ds(pl.multiple_of(start, HEAD), out.shape[1])
        copies.append(pltpu.make_async_copy(weight.at[:, where], out, sems.at[i]))
    for c in copies:
        c.start()
    for c in copies:
        c.wait()


def home_kernel(cap, blocks, gone_ref, *refs):
    gone = gone_ref[0]
    n = len(refs) // 3
    cots, backs, outs = refs[:n], refs[n : 2 * n], refs[2 * n :]
    for cot, out in zip(cots, outs):
        for b in range(blocks):
            start = pl.multiple_of((b - (b > gone).astype(jnp.int32)) * cap, cap)
            out[b * cap : (b + 1) * cap] = cot[pl.ds(start, cap), :]

    @pl.when(gone < blocks)
    def _():
        for back, out in zip(backs, outs):
            out[pl.ds(pl.multiple_of(gone * cap, cap), cap), :] = back[...]


def own_kernel(t_ref, cot_own, cot_sib, weight, out):
    part = cot_own.shape[1]
    t = t_ref[0]
    total = None
    for cot, i in ((cot_own, t), (cot_sib, t ^ 1)):
        start = pl.multiple_of(i * part, part)
        term = nt(cot[...], weight[:, pl.ds(start, part)])
        total = term if total is None else total + term
    out[...] = total


def by_place(t, place, own, sib, run):
    same = (t & 1) == (place >> 1)
    pl.when(same)(lambda: run(own, sib))
    pl.when(jnp.logical_not(same))(lambda: run(sib, own))


def far_kernel(t, place, cot_own, cot_sib, *refs):
    out, chunks = refs[-1], refs[:-1]
    chunks = [chunks[i : i + 3] for i in range(0, len(chunks), 3)]
    cols = sum(c[0].shape[1] for c in chunks)
    y = place[0] & 1

    def run(a, b):
        total = None
        at = 0
        for mine, by_y, by_z in chunks:
            size = mine.shape[1]
            near_at = pl.ds(pl.multiple_of(y * cols + at, HEAD), size)
            next_at = pl.ds(pl.multiple_of((1 - y) * cols + at, HEAD), size)
            term = nt(a[:, near_at], mine[...]) + nt(a[:, next_at], by_y[...])
            term += nt(b[:, near_at], by_z[...])
            total = term if total is None else total + term
            at += size
        out[...] = total

    by_place(t[0], place[0], cot_own, cot_sib, run)


def last_kernel(t, place, cot_own, cot_sib, part_sum, diag_a, diag_b, direct, out):
    cols = diag_a.shape[1]
    rest = direct.shape[1] // 2
    core = t[0] & 1
    at = pl.ds(pl.multiple_of((1 - (place[0] & 1)) * cols, HEAD), cols)
    own_at = pl.ds(pl.multiple_of(core * rest, HEAD), rest)
    sib_at = pl.ds(pl.multiple_of((1 - core) * rest, HEAD), rest)

    def run(a, b):
        diag = jnp.concatenate([diag_a[...], diag_b[...]], axis=0)
        total = part_sum[...] + nt(b[:, at], diag)
        total += nt(cot_own[:, 2 * cols :], direct[:, own_at])
        total += nt(cot_sib[:, 2 * cols :], direct[:, sib_at])
        out[...] = total.astype(BF16)

    by_place(t[0], place[0], cot_own, cot_sib, run)


def fill_left(cap, gone, att, far_att, left):
    rows, width = att.shape
    last = rows - 2 * cap
    swap = gone * cap < rows - cap
    for i, src in enumerate((att, far_att)):
        where = slice(i * width, (i + 1) * width)
        left[:last, where] = src[:last]
        home, came = src[last : rows - cap, :], src[rows - cap :, :]
        left[last : rows - cap, where] = jnp.where(swap, came, home)
        left[rows - cap :, where] = jnp.where(swap, home, came)


def early_kernel(cap, part, gone, t_ref, place_ref, att, far_att, weight, *refs):
    own_out, sib_out, left = refs[-3:]
    chunks = [refs[i : i + 3] for i in range(0, len(refs) - 3, 3)]
    t, place = t_ref[0], place_ref[0]
    y, z = place & 1, place >> 1
    cols = own_out.shape[1] // 2
    fill_left(cap, gone[0], att, far_att, left)

    def run(a, b):
        at = 0
        for mine, by_y, by_z in chunks:
            size = mine.shape[1]
            for out, k, j, far_weight in (
                (a, z, y, mine),
                (a, z, 1 - y, by_y),
                (b, 1 - z, y, by_z),
            ):
                start = pl.multiple_of(((t >> 1) * 2 + k) * part + j * cols + at, HEAD)
                both = jnp.concatenate([weight[:, pl.ds(start, size)], far_weight[...]], axis=0)
                here = pl.ds(pl.multiple_of(j * cols + at, HEAD), size)
                out[:, here] = nn(left[...], both).astype(BF16)
            at += size

    by_place(t, place, own_out, sib_out, run)


def late_kernel(t_ref, place_ref, left, weight, diag_a, diag_b, direct, own_out, sib_out):
    t, place = t_ref[0], place_ref[0]
    core, y, z = t & 1, place & 1, place >> 1
    part = weight.shape[1] // 4
    cols = diag_a.shape[1]
    rest = direct.shape[1] // 2

    def product(k, at, size, *far_weight):
        start = pl.multiple_of(((t >> 1) * 2 + k) * part + at, HEAD)
        both = jnp.concatenate([weight[:, pl.ds(start, size)], *far_weight], axis=0)
        return nn(left[...], both).astype(BF16)

    value = product(1 - z, (1 - y) * cols, cols, diag_a[...], diag_b[...])
    own_out[:, :cols] = value
    sib_out[:, :cols] = value
    for out, k in ((own_out, core), (sib_out, 1 - core)):
        where = pl.ds(pl.multiple_of(k * rest, HEAD), rest)
        out[:, cols:] = product(k, 2 * cols, rest, direct[:, where])


def join_kernel(cap, t_ref, place_ref, own, other, own_late, other_late, out, buf, sems):
    t, place = t_ref[0], place_ref[0]
    y, z = place & 1, place >> 1
    cols = own.shape[1] // 2
    same = (t & 1) == z

    def add(a, b):
        return (a.astype(F32) + b.astype(F32)).astype(BF16)

    copies = []
    for i in range(own.shape[0] // cap):
        rows = slice(i * cap, (i + 1) * cap)

        @pl.when(same)
        def _(rows=rows):
            buf[rows, : 2 * cols] = add(own[rows], other[rows])

        @pl.when(jnp.logical_not(same))
        def _(rows=rows):
            here = pl.ds(pl.multiple_of(y * cols, HEAD), cols)
            buf[rows, here] = add(own[rows, here], other[rows, here])
            there = pl.ds(pl.multiple_of((1 - y) * cols, HEAD), cols)
            buf[rows, there] = add(own_late[rows, :cols], other_late[rows, :cols])

        buf[rows, 2 * cols :] = add(own_late[rows, cols:], other_late[rows, cols:])
        where = pl.ds(i * cap, cap)
        copy = pltpu.make_async_copy(buf.at[where, :], out.at[where, :], sems.at[i])
        copy.start()
        copies.append(copy)
    for copy in copies:
        copy.wait()


def backward_kernel(q, k, v, pt, near, far, gq, gk, gv, bq, bk, bv, sems):
    copies = []
    for h in range(q.shape[1] // HEAD):
        cols = slice(h * HEAD, (h + 1) * HEAD)
        where = pl.ds(h * HEAD, HEAD)

        def send(buf, out, n, where=where, h=h):
            copy = pltpu.make_async_copy(buf.at[:, where], out.at[:, where], sems.at[3 * h + n])
            copy.start()
            copies.append(copy)

        cot = (near[:, cols] + far[:, cols].astype(F32)).astype(BF16)
        weights = pt[h]
        bv[:, cols] = nn(weights, cot).astype(BF16)
        send(bv, gv, 0)
        rise = nt(v[:, cols], cot)
        wide = weights.astype(F32)
        mean = jnp.sum(wide * rise, axis=0, keepdims=True)
        slope = (wide * (rise - mean) * HEAD ** (-0.5)).astype(BF16)
        bk[:, cols] = nn(slope, q[:, cols]).astype(BF16)
        send(bk, gk, 1)
        bq[:, cols] = tn(slope, k[:, cols]).astype(BF16)
        send(bq, gq, 2)
    for copy in copies:
        copy.wait()


def gradients(queries, key_rows, value_rows, pt, near, far, flops):
    home, width = queries.shape
    return call(
        backward_kernel,
        [((home, width), BF16)] * 3,
        [VMEM] * 6,
        [pltpu.VMEM((home, width), BF16)] * 3
        + [pltpu.SemaphoreType.DMA((3 * (width // HEAD),))],
        flops=flops,
        moved=9 * home * width * 2,
        out=ANY,
    )(queries, key_rows, value_rows, pt, near, far)


def flip(values, axis, by):
    size = lax.axis_size(axis)
    return lax.ppermute(values, axis, [(i, i ^ by) for i in range(size)])


def shifted(values, axis, by):
    size = lax.axis_size(axis)
    return lax.ppermute(values, axis, [(i, (i + by) % size) for i in range(size)])


def tie(value, *others):
    return lax.optimization_barrier((value, *others))[0]


def shards(queries, key_rows, value_rows, out_weight, segment_ids, move_flags, out_cotangent):
    home, width = queries.shape
    dest, part = out_cotangent.shape
    cap = dest - home
    blocks = home // cap
    heads = width // HEAD
    cols = part * 5 // 12 // HEAD * HEAD
    rest = part - 2 * cols
    t = lax.axis_index("tensor").astype(jnp.int32).reshape(1)
    place = (lax.axis_index("dp").astype(jnp.int32) & 3).reshape(1)

    share, direct = call(
        functools.partial(share_kernel, part, cols),
        [((width, cols), BF16), ((width, 2 * rest), BF16)],
        [SMEM, SMEM, ANY],
        [pltpu.SemaphoreType.DMA((3,))],
        limit=OPEN_LIMIT,
    )(t, place, out_weight)
    first = flip(share, "tensor", 2)
    cot_raw = flip(out_cotangent, "tensor", 1)

    gone, picked, att, sent, pt = attend(
        tie(segment_ids, share), move_flags, queries, key_rows, value_rows, out_cotangent
    )
    back = shifted(picked, "dp", -1)
    came = shifted(sent, "dp", 1)

    first, back, came = lax.optimization_barrier((first, back, came))
    by_y = flip(first, "dp", 1)
    by_z = flip(first, "dp", 2)
    att = lax.dynamic_update_slice(att, came, (home, 0))
    far_att = flip(att, "tensor", 2)
    direct = flip(tie(direct, att), "tensor", 2)
    back_sib = flip(back, "tensor", 1)

    cot_own, cot_sib = call(
        functools.partial(home_kernel, cap, blocks),
        [((home, part), BF16)] * 2,
        [SMEM] + [VMEM] * 4,
    )(gone, out_cotangent, cot_raw, back, back_sib)

    near = call(
        own_kernel,
        [((home, width), F32)],
        [SMEM, VMEM, VMEM, VMEM],
        flops=4 * home * width * part,
        moved=(home + width) * part * 4,
    )(t, cot_own, cot_sib, out_weight)[0]

    by_y, near, far_att = lax.optimization_barrier((by_y, near, far_att))
    by_z = tie(by_z, near)
    rows_a = width * 240 // 384 // 16 * 16
    diag_a = flip(by_y[:rows_a], "dp", 2)
    diag_b = flip(by_z[rows_a:], "dp", 1)

    early = (first, by_y, by_z)
    half = call(
        far_kernel,
        [((home, width), F32)],
        [SMEM, SMEM] + [VMEM] * 5,
        flops=6 * home * width * cols,
        moved=(home + width) * cols * 6,
    )(t, place, cot_own, cot_sib, *early)[0]
    own, sib, left = call(
        functools.partial(early_kernel, cap, part),
        [((dest, 2 * cols), BF16), ((dest, 2 * cols), BF16), ((dest, 2 * width), BF16)],
        [SMEM] * 3 + [VMEM] * 6,
        flops=12 * dest * width * cols,
        moved=12 * width * cols + dest * part * 4,
    )(gone, t, place, att, far_att, out_weight, *early)
    other = flip(sib, "tensor", 1)
    half, own = lax.optimization_barrier((half, own))
    send = call(
        last_kernel,
        [((home, width), BF16)],
        [SMEM, SMEM] + [VMEM] * 6,
        flops=2 * home * width * (cols + 2 * rest),
        moved=(home + width) * (cols + 2 * rest) * 2,
    )(t, place, cot_own, cot_sib, half, diag_a, diag_b, direct)[0]
    far = flip(send, "tensor", 2)
    own_late, sib_late = call(
        late_kernel,
        [((dest, cols + rest), BF16)] * 2,
        [SMEM] * 2 + [VMEM] * 5,
        flops=4 * dest * width * (cols + 2 * rest),
        moved=4 * width * (cols + 2 * rest) + dest * part * 2,
    )(t, tie(place, send), left, out_weight, diag_a, diag_b, direct)
    other_late = flip(sib_late, "tensor", 1)
    projected = call(
        functools.partial(join_kernel, cap),
        [((dest, part), BF16)],
        [SMEM] * 2 + [VMEM] * 4,
        [pltpu.VMEM((dest, part), BF16), pltpu.SemaphoreType.DMA((blocks + 1,))],
        moved=dest * part * 6,
        out=ANY,
    )(t, place, own, other, own_late, other_late)[0]

    grad_q, grad_k, grad_v = gradients(
        queries, key_rows, value_rows, pt, near, far, 800 * home * home * width
    )
    return (projected, grad_q, grad_k, grad_v)


def wide_shards(queries, key_rows, value_rows, out_weight, segment_ids, move_flags, out_cotangent):
    home, width = queries.shape
    dest, part = out_cotangent.shape
    cap = dest - home
    blocks = home // cap
    heads = width // HEAD
    gone, picked, att, sent, pt = attend(
        segment_ids, move_flags, queries, key_rows, value_rows, out_cotangent
    )
    came = shifted(sent, "dp", 1)
    kept = jnp.where(gone[0] < blocks, home - cap, home)
    att = lax.dynamic_update_slice(att, came, (kept, 0))
    term = jnp.dot(att, out_weight, preferred_element_type=F32).astype(BF16)
    projected = lax.psum_scatter(term, "tensor", scatter_dimension=1, tiled=True)
    back = shifted(picked, "dp", -1)
    cot = call(
        functools.partial(home_kernel, cap, blocks),
        [((home, part), BF16)],
        [SMEM, VMEM, VMEM],
    )(gone, out_cotangent, back)[0]
    whole = lax.all_gather(cot, "tensor", axis=1, tiled=True)
    near = nt(whole, out_weight)
    none = jnp.zeros((home, width), BF16)
    grad_q, grad_k, grad_v = gradients(queries, key_rows, value_rows, pt, near, none, 0)
    return (projected, grad_q, grad_k, grad_v)


def solution(mesh):
    square = mesh.shape["tensor"] == 4 and mesh.shape["dp"] % 4 == 0
    in_specs = (
        P("dp", "tensor"),
        P("dp", "tensor"),
        P("dp", "tensor"),
        P("tensor", None),
        P("dp", None),
        P("dp", None),
        P("dp", "tensor"),
    )
    out_specs = (P("dp", "tensor"), P("dp", "tensor"), P("dp", "tensor"), P("dp", "tensor"))
    return jax.shard_map(
        shards if square else wide_shards,
        mesh=mesh,
        in_specs=in_specs,
        out_specs=out_specs,
        check_vma=False,
    )
```

```python
import functools

import jax
import jax.numpy as jnp
from jax import lax
from jax.experimental import pallas as pl
from jax.experimental.pallas import tpu as pltpu
from jax.sharding import PartitionSpec as P

HEAD = 128
BF16 = jnp.bfloat16
F32 = jnp.float32
VMEM = pl.BlockSpec(memory_space=pltpu.VMEM)
SMEM = pl.BlockSpec(memory_space=pltpu.SMEM)
ANY = pl.BlockSpec(memory_space=pl.ANY)
LIMIT = 16 * 1024 * 1024
OPEN_LIMIT = 52 * 1024 * 1024


def nt(a, b):
    return lax.dot_general(a, b, (((1,), (1,)), ((), ())), preferred_element_type=F32)


def nn(a, b):
    return lax.dot_general(a, b, (((1,), (0,)), ((), ())), preferred_element_type=F32)


def tn(a, b):
    return lax.dot_general(a, b, (((0,), (0,)), ((), ())), preferred_element_type=F32)


def call(kernel, outs, ins, scratch=(), flops=0, moved=0, exps=0, limit=LIMIT, out=None):
    return pl.pallas_call(
        kernel,
        out_shape=tuple(jax.ShapeDtypeStruct(s, t) for s, t in outs),
        in_specs=list(ins),
        out_specs=tuple(out or (SMEM if t == jnp.int32 else VMEM) for _, t in outs),
        scratch_shapes=list(scratch),
        compiler_params=pltpu.CompilerParams(vmem_limit_bytes=limit),
        cost_estimate=pl.CostEstimate(flops=flops, bytes_accessed=moved, transcendentals=exps),
    )


def moved_block(seg, flags, blocks, cap):
    out = jnp.int32(blocks)
    for b in range(blocks):
        out = jnp.where(flags[0, seg[0, b * cap]] == 1, jnp.int32(b), out)
    return out


def attend(segment_ids, move_flags, queries, key_rows, value_rows, out_cotangent):
    home, width = queries.shape
    dest, part = out_cotangent.shape
    cap = dest - home
    return call(
        functools.partial(forward_kernel, cap),
        [
            ((1,), jnp.int32),
            ((cap, part), BF16),
            ((dest, width), BF16),
            ((cap, width), BF16),
            ((width // HEAD, home, home), BF16),
        ],
        [SMEM, SMEM] + [VMEM] * 4,
        [pltpu.VMEM((home // cap + 1, cap, width), BF16)],
    )(segment_ids, move_flags, queries, key_rows, value_rows, out_cotangent)


def forward_kernel(cap, seg, flags, q, k, v, cot, gone_out, picked, att, sent, pt, rows_buf):
    rows, width = q.shape
    blocks = rows // cap
    gone = moved_block(seg, flags, blocks, cap)
    gone_out[0] = gone
    row = jnp.where(gone == blocks, blocks, blocks - 1)
    picked[...] = cot[pl.ds(pl.multiple_of(row * cap, cap), cap), :]
    col_block = lax.broadcasted_iota(jnp.int32, (rows, 1), 0) // cap
    row_block = lax.broadcasted_iota(jnp.int32, (1, rows), 1) // cap
    key_id = jnp.zeros((rows, 1), jnp.int32)
    query_id = jnp.zeros((1, rows), jnp.int32)
    for b in range(blocks):
        image = seg[0, b * cap]
        key_id = jnp.where(col_block == b, image, key_id)
        query_id = jnp.where(row_block == b, image, query_id)
    same = key_id == query_id
    for h in range(width // HEAD):
        cols = slice(h * HEAD, (h + 1) * HEAD)
        scores = nt(k[:, cols], q[:, cols]) * HEAD ** (-0.5)
        scores = jnp.where(same, scores, -1e30)
        weights = jnp.exp(scores - jnp.max(scores, axis=0, keepdims=True))
        weights = weights * (1.0 / jnp.sum(weights, axis=0, keepdims=True))
        weights = weights.astype(BF16)
        pt[h] = weights
        out = tn(weights, v[:, cols]).astype(BF16)
        for b in range(blocks):
            slot = jnp.where(b < gone, b, jnp.where(b == gone, blocks, b - 1))
            rows_buf[slot, :, cols] = out[b * cap : (b + 1) * cap]
    empty = jnp.where(gone == blocks, blocks, blocks - 1)
    rows_buf[empty] = jnp.zeros((cap, width), BF16)
    for b in range(blocks):
        att[b * cap : (b + 1) * cap] = rows_buf[b]
    att[rows:] = jnp.zeros((cap, width), BF16)
    sent[...] = rows_buf[blocks]


def share_kernel(part, cols, t, place, weight, *refs):
    outs, direct, sems = refs[:-2], refs[-2], refs[-1]
    rest = direct.shape[1] // 2
    far = (1 - (t[0] >> 1)) * 2 * part
    at = far + (place[0] >> 1) * part + (place[0] & 1) * cols
    moves = []
    for out in outs:
        moves.append((at, out))
        at += out.shape[1]
    for k in range(2):
        moves.append((far + (k + 1) * part - rest, direct.at[:, pl.ds(k * rest, rest)]))
    copies = []
    for i, (start, out) in enumerate(moves):
        where = pl.ds(pl.multiple_of(start, HEAD), out.shape[1])
        copies.append(pltpu.make_async_copy(weight.at[:, where], out, sems.at[i]))
    for c in copies:
        c.start()
    for c in copies:
        c.wait()


def home_kernel(cap, blocks, gone_ref, *refs):
    gone = gone_ref[0]
    n = len(refs) // 3
    cots, backs, outs = refs[:n], refs[n : 2 * n], refs[2 * n :]
    for cot, out in zip(cots, outs):
        for b in range(blocks):
            start = pl.multiple_of((b - (b > gone).astype(jnp.int32)) * cap, cap)
            out[b * cap : (b + 1) * cap] = cot[pl.ds(start, cap), :]

    @pl.when(gone < blocks)
    def _():
        for back, out in zip(backs, outs):
            out[pl.ds(pl.multiple_of(gone * cap, cap), cap), :] = back[...]


def own_kernel(t_ref, cot_own, cot_sib, weight, out):
    part = cot_own.shape[1]
    t = t_ref[0]
    total = None
    for cot, i in ((cot_own, t), (cot_sib, t ^ 1)):
        start = pl.multiple_of(i * part, part)
        term = nt(cot[...], weight[:, pl.ds(start, part)])
        total = term if total is None else total + term
    out[...] = total


def by_place(t, place, own, sib, run):
    same = (t & 1) == (place >> 1)
    pl.when(same)(lambda: run(own, sib))
    pl.when(jnp.logical_not(same))(lambda: run(sib, own))


def far_kernel(t, place, cot_own, cot_sib, *refs):
    out, chunks = refs[-1], refs[:-1]
    chunks = [chunks[i : i + 3] for i in range(0, len(chunks), 3)]
    cols = sum(c[0].shape[1] for c in chunks)
    y = place[0] & 1

    def run(a, b):
        total = None
        at = 0
        for mine, by_y, by_z in chunks:
            size = mine.shape[1]
            near_at = pl.ds(pl.multiple_of(y * cols + at, HEAD), size)
            next_at = pl.ds(pl.multiple_of((1 - y) * cols + at, HEAD), size)
            term = nt(a[:, near_at], mine[...]) + nt(a[:, next_at], by_y[...])
            term += nt(b[:, near_at], by_z[...])
            total = term if total is None else total + term
            at += size
        out[...] = total

    by_place(t[0], place[0], cot_own, cot_sib, run)


def last_kernel(t, place, cot_own, cot_sib, part_sum, diag_a, diag_b, direct, out):
    cols = diag_a.shape[1]
    rest = direct.shape[1] // 2
    core = t[0] & 1
    at = pl.ds(pl.multiple_of((1 - (place[0] & 1)) * cols, HEAD), cols)
    own_at = pl.ds(pl.multiple_of(core * rest, HEAD), rest)
    sib_at = pl.ds(pl.multiple_of((1 - core) * rest, HEAD), rest)

    def run(a, b):
        diag = jnp.concatenate([diag_a[...], diag_b[...]], axis=0)
        total = part_sum[...] + nt(b[:, at], diag)
        total += nt(cot_own[:, 2 * cols :], direct[:, own_at])
        total += nt(cot_sib[:, 2 * cols :], direct[:, sib_at])
        out[...] = total.astype(BF16)

    by_place(t[0], place[0], cot_own, cot_sib, run)


def fill_left(cap, gone, att, far_att, left):
    rows, width = att.shape
    last = rows - 2 * cap
    swap = gone * cap < rows - cap
    for i, src in enumerate((att, far_att)):
        where = slice(i * width, (i + 1) * width)
        left[:last, where] = src[:last]
        home, came = src[last : rows - cap, :], src[rows - cap :, :]
        left[last : rows - cap, where] = jnp.where(swap, came, home)
        left[rows - cap :, where] = jnp.where(swap, home, came)


def early_kernel(cap, part, gone, t_ref, place_ref, att, far_att, weight, *refs):
    own_out, sib_out, left = refs[-3:]
    chunks = [refs[i : i + 3] for i in range(0, len(refs) - 3, 3)]
    t, place = t_ref[0], place_ref[0]
    y, z = place & 1, place >> 1
    cols = own_out.shape[1] // 2
    fill_left(cap, gone[0], att, far_att, left)

    def run(a, b):
        at = 0
        for mine, by_y, by_z in chunks:
            size = mine.shape[1]
            for out, k, j, far_weight in (
                (a, z, y, mine),
                (a, z, 1 - y, by_y),
                (b, 1 - z, y, by_z),
            ):
                start = pl.multiple_of(((t >> 1) * 2 + k) * part + j * cols + at, HEAD)
                both = jnp.concatenate([weight[:, pl.ds(start, size)], far_weight[...]], axis=0)
                here = pl.ds(pl.multiple_of(j * cols + at, HEAD), size)
                out[:, here] = nn(left[...], both).astype(BF16)
            at += size

    by_place(t, place, own_out, sib_out, run)


def late_kernel(t_ref, place_ref, left, weight, diag_a, diag_b, direct, own_out, sib_out):
    t, place = t_ref[0], place_ref[0]
    core, y, z = t & 1, place & 1, place >> 1
    part = weight.shape[1] // 4
    cols = diag_a.shape[1]
    rest = direct.shape[1] // 2

    def product(k, at, size, *far_weight):
        start = pl.multiple_of(((t >> 1) * 2 + k) * part + at, HEAD)
        both = jnp.concatenate([weight[:, pl.ds(start, size)], *far_weight], axis=0)
        return nn(left[...], both).astype(BF16)

    value = product(1 - z, (1 - y) * cols, cols, diag_a[...], diag_b[...])
    own_out[:, :cols] = value
    sib_out[:, :cols] = value
    for out, k in ((own_out, core), (sib_out, 1 - core)):
        where = pl.ds(pl.multiple_of(k * rest, HEAD), rest)
        out[:, cols:] = product(k, 2 * cols, rest, direct[:, where])


def join_kernel(cap, t_ref, place_ref, own, other, own_late, other_late, out, buf, sems):
    t, place = t_ref[0], place_ref[0]
    y, z = place & 1, place >> 1
    cols = own.shape[1] // 2
    same = (t & 1) == z

    def add(a, b):
        return (a.astype(F32) + b.astype(F32)).astype(BF16)

    copies = []
    for i in range(own.shape[0] // cap):
        rows = slice(i * cap, (i + 1) * cap)

        @pl.when(same)
        def _(rows=rows):
            buf[rows, : 2 * cols] = add(own[rows], other[rows])

        @pl.when(jnp.logical_not(same))
        def _(rows=rows):
            here = pl.ds(pl.multiple_of(y * cols, HEAD), cols)
            buf[rows, here] = add(own[rows, here], other[rows, here])
            there = pl.ds(pl.multiple_of((1 - y) * cols, HEAD), cols)
            buf[rows, there] = add(own_late[rows, :cols], other_late[rows, :cols])

        buf[rows, 2 * cols :] = add(own_late[rows, cols:], other_late[rows, cols:])
        where = pl.ds(i * cap, cap)
        copy = pltpu.make_async_copy(buf.at[where, :], out.at[where, :], sems.at[i])
        copy.start()
        copies.append(copy)
    for copy in copies:
        copy.wait()


def backward_kernel(q, k, v, pt, near, far, gq, gk, gv, bq, bk, bv, sems):
    copies = []
    for h in range(q.shape[1] // HEAD):
        cols = slice(h * HEAD, (h + 1) * HEAD)
        where = pl.ds(h * HEAD, HEAD)

        def send(buf, out, n, where=where, h=h):
            copy = pltpu.make_async_copy(buf.at[:, where], out.at[:, where], sems.at[3 * h + n])
            copy.start()
            copies.append(copy)

        cot = (near[:, cols] + far[:, cols].astype(F32)).astype(BF16)
        weights = pt[h]
        rise = nt(v[:, cols], cot)
        wide = weights.astype(F32)
        mean = jnp.sum(wide * rise, axis=0, keepdims=True)
        slope = (wide * (rise - mean) * HEAD ** (-0.5)).astype(BF16)
        bv[:, cols] = nn(weights, cot).astype(BF16)
        send(bv, gv, 0)
        bk[:, cols] = nn(slope, q[:, cols]).astype(BF16)
        send(bk, gk, 1)
        bq[:, cols] = tn(slope, k[:, cols]).astype(BF16)
        send(bq, gq, 2)
    for copy in copies:
        copy.wait()


def gradients(queries, key_rows, value_rows, pt, near, far, flops):
    home, width = queries.shape
    return call(
        backward_kernel,
        [((home, width), BF16)] * 3,
        [VMEM] * 6,
        [pltpu.VMEM((home, width), BF16)] * 3
        + [pltpu.SemaphoreType.DMA((3 * (width // HEAD),))],
        flops=flops,
        moved=9 * home * width * 2,
        out=ANY,
    )(queries, key_rows, value_rows, pt, near, far)


def flip(values, axis, by):
    size = lax.axis_size(axis)
    return lax.ppermute(values, axis, [(i, i ^ by) for i in range(size)])


def shifted(values, axis, by):
    size = lax.axis_size(axis)
    return lax.ppermute(values, axis, [(i, (i + by) % size) for i in range(size)])


def tie(value, *others):
    return lax.optimization_barrier((value, *others))[0]


def shards(queries, key_rows, value_rows, out_weight, segment_ids, move_flags, out_cotangent):
    home, width = queries.shape
    dest, part = out_cotangent.shape
    cap = dest - home
    blocks = home // cap
    heads = width // HEAD
    cols = part * 5 // 12 // HEAD * HEAD
    rest = part - 2 * cols
    t = lax.axis_index("tensor").astype(jnp.int32).reshape(1)
    place = (lax.axis_index("dp").astype(jnp.int32) & 3).reshape(1)

    share, direct = call(
        functools.partial(share_kernel, part, cols),
        [((width, cols), BF16), ((width, 2 * rest), BF16)],
        [SMEM, SMEM, ANY],
        [pltpu.SemaphoreType.DMA((3,))],
        limit=OPEN_LIMIT,
    )(t, place, out_weight)
    first = flip(share, "tensor", 2)
    cot_raw = flip(out_cotangent, "tensor", 1)

    gone, picked, att, sent, pt = attend(
        tie(segment_ids, share), move_flags, queries, key_rows, value_rows, out_cotangent
    )
    back = shifted(picked, "dp", -1)
    came = shifted(sent, "dp", 1)

    first, back, came = lax.optimization_barrier((first, back, came))
    by_y = flip(first, "dp", 1)
    by_z = flip(first, "dp", 2)
    att = lax.dynamic_update_slice(att, came, (home, 0))
    far_att = flip(att, "tensor", 2)
    direct = flip(tie(direct, att), "tensor", 2)
    back_sib = flip(back, "tensor", 1)

    cot_own, cot_sib = call(
        functools.partial(home_kernel, cap, blocks),
        [((home, part), BF16)] * 2,
        [SMEM] + [VMEM] * 4,
    )(gone, out_cotangent, cot_raw, back, back_sib)

    near = call(
        own_kernel,
        [((home, width), F32)],
        [SMEM, VMEM, VMEM, VMEM],
        flops=4 * home * width * part,
        moved=(home + width) * part * 4,
    )(t, cot_own, cot_sib, out_weight)[0]

    by_y, near, far_att = lax.optimization_barrier((by_y, near, far_att))
    by_z = tie(by_z, near)
    rows_a = width * 7 // 12 // 32 * 32
    diag_a = flip(by_y[:rows_a], "dp", 2)
    diag_b = flip(by_z[rows_a:], "dp", 1)

    early = (first, by_y, by_z)
    half = call(
        far_kernel,
        [((home, width), F32)],
        [SMEM, SMEM] + [VMEM] * 5,
        flops=6 * home * width * cols,
        moved=(home + width) * cols * 6,
    )(t, place, cot_own, cot_sib, *early)[0]
    send = call(
        last_kernel,
        [((home, width), BF16)],
        [SMEM, SMEM] + [VMEM] * 6,
        flops=2 * home * width * (cols + 2 * rest),
        moved=(home + width) * (cols + 2 * rest) * 2,
    )(t, place, cot_own, cot_sib, half, diag_a, diag_b, direct)[0]
    far = flip(send, "tensor", 2)
    own, sib, left = call(
        functools.partial(early_kernel, cap, part),
        [((dest, 2 * cols), BF16), ((dest, 2 * cols), BF16), ((dest, 2 * width), BF16)],
        [SMEM] * 3 + [VMEM] * 6,
        flops=12 * dest * width * cols,
        moved=12 * width * cols + dest * part * 4,
    )(gone, t, tie(place, send), att, far_att, out_weight, *early)
    other = flip(sib, "tensor", 1)
    own_late, sib_late = call(
        late_kernel,
        [((dest, cols + rest), BF16)] * 2,
        [SMEM] * 2 + [VMEM] * 5,
        flops=4 * dest * width * (cols + 2 * rest),
        moved=4 * width * (cols + 2 * rest) + dest * part * 2,
    )(t, tie(place, send), left, out_weight, diag_a, diag_b, direct)
    other_late = flip(sib_late, "tensor", 1)
    projected = call(
        functools.partial(join_kernel, cap),
        [((dest, part), BF16)],
        [SMEM] * 2 + [VMEM] * 4,
        [pltpu.VMEM((dest, part), BF16), pltpu.SemaphoreType.DMA((blocks + 1,))],
        moved=dest * part * 6,
        out=ANY,
    )(t, place, own, other, own_late, other_late)[0]

    grad_q, grad_k, grad_v = gradients(
        queries, key_rows, value_rows, pt, near, far, 800 * home * home * width
    )
    return (projected, grad_q, grad_k, grad_v)


def wide_shards(queries, key_rows, value_rows, out_weight, segment_ids, move_flags, out_cotangent):
    home, width = queries.shape
    dest, part = out_cotangent.shape
    cap = dest - home
    blocks = home // cap
    heads = width // HEAD
    gone, picked, att, sent, pt = attend(
        segment_ids, move_flags, queries, key_rows, value_rows, out_cotangent
    )
    came = shifted(sent, "dp", 1)
    kept = jnp.where(gone[0] < blocks, home - cap, home)
    att = lax.dynamic_update_slice(att, came, (kept, 0))
    term = jnp.dot(att, out_weight, preferred_element_type=F32).astype(BF16)
    projected = lax.psum_scatter(term, "tensor", scatter_dimension=1, tiled=True)
    back = shifted(picked, "dp", -1)
    cot = call(
        functools.partial(home_kernel, cap, blocks),
        [((home, part), BF16)],
        [SMEM, VMEM, VMEM],
    )(gone, out_cotangent, back)[0]
    whole = lax.all_gather(cot, "tensor", axis=1, tiled=True)
    near = nt(whole, out_weight)
    none = jnp.zeros((home, width), BF16)
    grad_q, grad_k, grad_v = gradients(queries, key_rows, value_rows, pt, near, none, 0)
    return (projected, grad_q, grad_k, grad_v)


def solution(mesh):
    square = mesh.shape["tensor"] == 4 and mesh.shape["dp"] % 4 == 0
    in_specs = (
        P("dp", "tensor"),
        P("dp", "tensor"),
        P("dp", "tensor"),
        P("tensor", None),
        P("dp", None),
        P("dp", None),
        P("dp", "tensor"),
    )
    out_specs = (P("dp", "tensor"), P("dp", "tensor"), P("dp", "tensor"), P("dp", "tensor"))
    return jax.shard_map(
        shards if square else wide_shards,
        mesh=mesh,
        in_specs=in_specs,
        out_specs=out_specs,
        check_vma=False,
    )
```
